256 devices in a mesh: dp: 16 (over x_lo, y, core), ctx: 16 (over x_hi, z).
Axes of the slice: x: 4 (x_hi: 2, x_lo: 2; x = x_hi * 2 + x_lo), y: 4, z: 8, core: 2. Of those that a mesh axis runs over, the one named last changes fastest.
Arguments:
- q_latent: bfloat16 [16, 2048, 32768], P('dp', 'ctx'), may hold values from -15 to 15
- q_rope: bfloat16 [16, 2048, 4096], P('dp', 'ctx'), may hold values from -4 to 4
- latent_cache: bfloat16 [16, 3072, 512], P('dp', 'ctx'), may hold values from -4 to 4
- rope_keys: bfloat16 [16, 3072, 64], P('dp', 'ctx'), may hold values from -4 to 4
- up_weight: bfloat16 [64, 512, 128], P('ctx', 'dp'), may hold values from -0.25 to 0.25
- out_grad: bfloat16 [16, 2048, 8192], P('dp', 'ctx'), may hold values from -6 to 6
- block_ids: int32 [16, 32, 4], P('dp', 'ctx'), may hold values from 0 to 47, as said below
- block_counts: int32 [16, 32], P('dp', 'ctx'), may hold values from 1 to 4, as said below
- slab_offset: int32 [16], P('dp'), may hold values from 0 to 1024, as said below
Outputs:
- cache_grad: bfloat16 [16, 3072, 512], P('dp', 'ctx')
- rope_grad: bfloat16 [16, 3072, 64], P('dp', 'ctx')
- weight_grad: float32 [64, 512, 128], P('ctx', 'dp')
The draws below stay inside these ranges and needn't reach their ends.
Inputs may be any that keep to these rules, and one draw needn't show every extreme that they name: `slab_offset`: A multiple of 64; the queries lie inside the context. `block_ids`: for query block b of a sequence with offset o, entry 0 is the key block o / 64 + b; entries 1 to count - 1 are distinct key blocks before it; entries from count on repeat entry 0. `block_counts`: count = 1 + min(3, o / 64 + b) for query block b of a sequence with offset o.
All inputs are finite; a program needn't handle non-finite values.
Results may differ from the reference program's by a relative error of at most 0.022.
Values may be sent and summed in bfloat16 or wider, within the bound.
A program may use at most 192 MiB of HBM per device.

```python
import jax
import jax.numpy as jnp
from jax import lax

H = 64
LAT = 512
ROPE = 64
HD = 128
BLK = 64
SEL = 4
SEQS = 16
LEN = 3072
SLAB = 2048
NKB = 48
NQB = 32


def drawn_lists(key):
    key = jax.random.fold_in(key, 101)
    key_one, key_two, key_three = jax.random.split(key, 3)
    offsets = jax.random.randint(key_one, (SEQS,), 0, NKB - NQB + 1).astype(jnp.int32)
    farthest = jax.random.randint(key_three, (), 0, SEQS).astype(jnp.int32)
    seq_index = jnp.arange(SEQS, dtype=jnp.int32)
    offsets = jnp.where(seq_index == farthest, NKB - NQB, offsets)
    offsets = jnp.where(seq_index == (farthest + 1) % SEQS, 0, offsets).astype(jnp.int32)
    diagonal = offsets[:, None] + jnp.arange(NQB, dtype=jnp.int32)[None, :]
    candidate = jnp.arange(NKB, dtype=jnp.int32)
    random_score = jax.random.randint(key_two, (SEQS, NQB, NKB), 0, 65536).astype(jnp.int32)
    earlier = candidate[None, None, :] < diagonal[:, :, None]
    ranking = jnp.where(earlier, random_score * NKB + candidate[None, None, :], -1 - candidate[None, None, :])
    best_values, best_index = lax.top_k(ranking, SEL - 1)
    slot_index = jnp.arange(SEL - 1, dtype=jnp.int32)
    picked = jnp.where(slot_index[None, None, :] < diagonal[:, :, None], best_index.astype(jnp.int32), diagonal[:, :, None])
    block_list = jnp.concatenate([diagonal[:, :, None], picked], axis=2)
    valid = 1 + jnp.minimum(SEL - 1, diagonal)
    return (offsets, block_list, valid)


def draw_slab_offset(key, part):
    offsets, block_list, valid = drawn_lists(key)
    return offsets * BLK


def draw_block_ids(key, part):
    offsets, block_list, valid = drawn_lists(key)
    return block_list


def draw_block_counts(key, part):
    offsets, block_list, valid = drawn_lists(key)
    return valid


def draw_latent_cache(key, part):
    key = jax.random.fold_in(key, 1)
    return jnp.clip(jax.random.normal(key, (SEQS, LEN, LAT), jnp.float32), -4.0, 4.0).astype(jnp.bfloat16)


def draw_rope_keys(key, part):
    key = jax.random.fold_in(key, 2)
    return jnp.clip(jax.random.normal(key, (SEQS, LEN, ROPE), jnp.float32), -4.0, 4.0).astype(jnp.bfloat16)


def draw_q_latent(key, part):
    key = jax.random.fold_in(key, 3)
    return jnp.clip(jax.random.normal(key, (SEQS, SLAB, H * LAT), jnp.float32), -4.0, 4.0).astype(jnp.bfloat16)


def draw_q_rope(key, part):
    key = jax.random.fold_in(key, 4)
    return jnp.clip(jax.random.normal(key, (SEQS, SLAB, H * ROPE), jnp.float32), -4.0, 4.0).astype(jnp.bfloat16)


def level_of(rng, extent, pieces, least, high):
    def one(dim, blocks):
        steps = jax.random.uniform(jax.random.fold_in(jax.random.fold_in(rng, 6), dim), (blocks,), jnp.float32, least / len(pieces), high / len(pieces))
        return jnp.repeat(jnp.exp(steps), extent[dim] // blocks).reshape((-1,) + (1,) * (len(extent) - dim - 1))

    loudness = one(*pieces[0])
    for cut in pieces[1:]:
        loudness = loudness * one(*cut)
    return loudness


def centred(stream_key, shape, deviation, limit, pieces=(), kind=jnp.bfloat16):
    result = deviation * jax.random.normal(stream_key, shape, jnp.float32)
    if pieces:
        result = result * level_of(stream_key, shape, pieces, -0.22, 0.18)
    return jnp.clip(result, -limit, limit).astype(kind)


def setup_inputs(seed: int = 0) -> dict:
    streams_of = jax.random.split(jax.random.key(seed), 10)
    return {
        "q_latent": draw_q_latent(jax.random.fold_in(streams_of[9], 71), 0),
        "q_rope": draw_q_rope(jax.random.fold_in(streams_of[9], 71), 0),
        "latent_cache": draw_latent_cache(jax.random.fold_in(streams_of[9], 71), 0),
        "rope_keys": draw_rope_keys(jax.random.fold_in(streams_of[9], 71), 0),
        "up_weight": centred(streams_of[4], (H, LAT, HD), LAT ** -0.5, 0.25, ((0, 16), (1, 16))),
        "out_grad": centred(streams_of[5], (SEQS, SLAB, H * HD), 1.0, 6.0, ((0, 16), (1, 16))),
        "block_ids": draw_block_ids(jax.random.fold_in(streams_of[9], 71), 0),
        "block_counts": draw_block_counts(jax.random.fold_in(streams_of[9], 71), 0),
        "slab_offset": draw_slab_offset(jax.random.fold_in(streams_of[9], 71), 0),
    }


def one_sequence(q_lat, q_rot, cache_full, rope_full, grad_out, weight, block_list, block_valid, offset):
    score_scale = (HD + ROPE) ** -0.5
    within = jnp.arange(BLK, dtype=jnp.int32)
    key_index = (block_list[:, :, None] * BLK + within[None, None, :]).reshape(NQB, SEL * BLK)
    key_tiles = cache_full[key_index].astype(jnp.float32)
    rope_tiles = rope_full[key_index].astype(jnp.float32)
    q_tiles = q_lat.reshape(NQB, BLK, H, LAT).astype(jnp.float32)
    qrope_tiles = q_rot.reshape(NQB, BLK, H, ROPE).astype(jnp.float32)
    scores = (jnp.einsum("bthl,bkl->bthk", q_tiles, key_tiles) + jnp.einsum("bthr,bkr->bthk", qrope_tiles, rope_tiles)) * score_scale
    positions = offset + jnp.arange(SLAB, dtype=jnp.int32).reshape(NQB, BLK)
    slot_index = jnp.arange(SEL * BLK, dtype=jnp.int32) // BLK
    visible = (slot_index[None, None, :] < block_valid[:, None, None]) & (key_index[:, None, :] <= positions[:, :, None])
    scores = jnp.where(visible[:, :, None, :], scores, -1e30)
    row_top = jnp.max(scores, axis=-1, keepdims=True)
    raw_weights = jnp.exp(scores - row_top)
    attention = raw_weights / jnp.sum(raw_weights, axis=-1, keepdims=True)
    attn_half = lax.optimization_barrier(attention.astype(jnp.bfloat16)).astype(jnp.float32)
    out_latent = jnp.einsum("bthk,bkl->bthl", attn_half, key_tiles).astype(jnp.bfloat16)
    out_flat = lax.optimization_barrier(out_latent).astype(jnp.float32).reshape(SLAB, H, LAT)
    grad_heads = grad_out.reshape(SLAB, H, HD).astype(jnp.float32)
    weight_part = jnp.einsum("thl,thd->hld", out_flat, grad_heads)
    latent_back = jnp.einsum("thd,hld->thl", grad_heads, weight.astype(jnp.float32)).astype(jnp.bfloat16)
    grad_latent = lax.optimization_barrier(latent_back).astype(jnp.float32).reshape(NQB, BLK, H, LAT)
    prob_back = jnp.einsum("bthl,bkl->bthk", grad_latent, key_tiles)
    row_delta = jnp.sum(attention * prob_back, axis=-1, keepdims=True)
    score_back = (attention * (prob_back - row_delta)).astype(jnp.bfloat16)
    score_back = lax.optimization_barrier(score_back).astype(jnp.float32)
    grad_key = jnp.einsum("bthk,bthl->bkl", attn_half, grad_latent) + score_scale * jnp.einsum("bthk,bthl->bkl", score_back, q_tiles)
    grad_rope = score_scale * jnp.einsum("bthk,bthr->bkr", score_back, qrope_tiles)
    flat_index = key_index.reshape(-1)
    cache_sum = jnp.zeros((LEN, LAT), jnp.float32).at[flat_index].add(grad_key.reshape(-1, LAT))
    rope_sum = jnp.zeros((LEN, ROPE), jnp.float32).at[flat_index].add(grad_rope.reshape(-1, ROPE))
    return cache_sum.astype(jnp.bfloat16), rope_sum.astype(jnp.bfloat16), weight_part


def reference(q_latent, q_rope, latent_cache, rope_keys, up_weight, out_grad, block_ids, block_counts, slab_offset):
    def advance(running, per_seq):
        q_lat, q_rot, cache_full, rope_full, grad_out, block_list, block_valid, offset = per_seq
        cache_part, rope_part, weight_part = one_sequence(q_lat, q_rot, cache_full, rope_full, grad_out, up_weight, block_list, block_valid, offset)
        return running + weight_part, (cache_part, rope_part)

    start_sum = jnp.zeros((H, LAT, HD), jnp.float32)
    weight_sum, (cache_grad, rope_grad) = lax.scan(advance, start_sum, (q_latent, q_rope, latent_cache, rope_keys, out_grad, block_ids, block_counts, slab_offset))
    return cache_grad, rope_grad, weight_sum
```

```python
import functools

import jax
import jax.numpy as jnp
from jax import lax
from jax.experimental import pallas as pl
from jax.experimental.pallas import tpu as pltpu
from jax.sharding import PartitionSpec as P

LAT = 512
ROPE = 64
HD = 128
BLK = 64
SEL = 4
SCALE = (HD + ROPE) ** (-0.5)
ROWS = 224
HALF = ROWS // 2
MESH = pl.DeviceIdType.MESH
BF = jnp.bfloat16
F32 = jnp.float32


def place():
    dp, ctx = lax.axis_index("dp"), lax.axis_index("ctx")
    core, y, x_lo = dp % 2, (dp // 2) % 4, dp // 8
    x_hi, z = ctx // 8, ctx % 8
    return x_hi * 2 + x_lo, y, z, core, x_hi


def device(x, y, z, core):
    return (((x % 2) * 4 + y) * 2 + core, (x // 2) * 8 + z)


class Links:
    def __init__(self, send, recv):
        x, y, z, core, _ = place()
        self.send, self.recv, self.count, self.started = send, recv, 0, []
        self.to = {
            "z": (device(x, y, (z + 1) % 8, core), device(x, y, (z + 7) % 8, core)),
            "y": (device(x, (y + 1) % 4, z, core), device(x, (y + 3) % 4, z, core)),
            "x": (device((x + 1) % 4, y, z, core), device((x + 3) % 4, y, z, core)),
            "far": (device((x + 2) % 4, y, z, core),),
            "core": (device(x, y, z, 1 - core),),
        }

    def barrier(self):
        sem = pltpu.get_barrier_semaphore()
        partners = [d for way in self.to.values() for d in way]
        for d in partners:
            pl.semaphore_signal(sem, inc=1, device_id=d, device_id_type=MESH)
        pl.semaphore_wait(sem, len(partners))

    def push(self, src, dst, way, side=0):
        i = self.count
        self.count += 1
        copy = pltpu.make_async_remote_copy(
            src_ref=src,
            dst_ref=dst,
            send_sem=self.send.at[i],
            recv_sem=self.recv.at[i],
            device_id=self.to[way][side],
            device_id_type=MESH,
        )
        copy.start()
        self.started.append(copy)
        return copy

    def finish(self):
        for copy in self.started:
            copy.wait_send()


def arrive(copies):
    for copy in copies:
        copy.wait_recv()


N_GATHER = 80
N_REDUCE = 80


def gather_kernel(cache_ref, rope_ref, w_ref, kc, g, blk, send, recv, lsem):
    x, y, z, core, xh = place()
    links = Links(send, recv)
    blk[0:192, :] = cache_ref[...]
    packed = [rope_ref[32 * i : 32 * i + 32, :] for i in range(6)]
    blk[192:224, :] = jnp.concatenate(packed + [jnp.zeros((32, 128), BF)], axis=1)
    links.barrier()

    def piece(part, zo):
        return g.at[0, core, y, x, zo] if part == 0 else g.at[1, core, x, y, zo]

    def w_step(s):
        out = []
        for side, sign in ((0, 1), (1, -1)):
            zo = (z - sign * (s - 1) + 8) % 8
            for part in (0, 1):
                src = w_ref.at[part] if s == 1 else piece(part, zo)
                dst = piece(part, zo)
                if s == 4:
                    rows = pl.ds(32 * side, 32)
                    src, dst = src.at[rows], dst.at[rows]
                out.append(links.push(src, dst, "z", side))
        return out

    def c_step(hf, s):
        out = []
        for side, sign in ((0, 1), (1, -1)):
            zo = (z - sign * (s - 1) + 8) % 8
            src = blk if (s == 1 and hf is xh) else kc.at[hf, zo]
            dst = kc.at[hf, zo]
            if s == 4:
                rows = pl.ds(HALF * side, HALF)
                src, dst = src.at[rows], dst.at[rows]
            out.append(links.push(src, dst, "z", side))
        return out

    def ring4(part, way, s, level):
        me = x if way == "x" else y
        out = []
        for side, sign in ((0, 1), (1, -1)):
            o = me if s == 1 else (me - sign + 4) % 4
            if level == 1:
                ref = g.at[part, core, y if part == 0 else x, o]
                if s == 2:
                    ref = ref.at[pl.ds(4 * side, 4)]
            else:
                ref = g.at[part, core, o]
                if s == 2:
                    ref = ref.at[pl.ds(2 * side, 2)]
            out.append(links.push(ref, ref, way, side))
        return out

    other = 1 - xh
    wz = w_step(1)
    c0 = c_step(xh, 1)
    cross = links.push(blk, kc.at[xh, z], "far")
    local = [
        pltpu.make_async_copy(blk, kc.at[xh, z], lsem.at[0]),
        pltpu.make_async_copy(w_ref.at[0], piece(0, z), lsem.at[1]),
        pltpu.make_async_copy(w_ref.at[1], piece(1, z), lsem.at[2]),
    ]
    for copy in local:
        copy.start()
    arrive(wz)
    wz = w_step(2)
    arrive(wz)
    wz = w_step(3)
    arrive(wz)
    wz = w_step(4)
    arrive(c0)
    c0 = c_step(xh, 2)
    arrive(wz)
    for copy in local:
        copy.wait()
    a, b = ring4(0, "x", 1, 1), ring4(1, "y", 1, 1)
    arrive([cross])
    c1 = c_step(other, 1)
    arrive(a)
    a = ring4(0, "x", 2, 1)
    arrive(b)
    b = ring4(1, "y", 2, 1)
    arrive(a)
    a = ring4(0, "y", 1, 2)
    arrive(b)
    b = ring4(1, "x", 1, 2)
    mine = (y, x)
    shared = []

    def share(part, o):
        ref = g.at[part, core, o]
        shared.append(links.push(ref, ref, "core"))

    share(0, y)
    share(1, x)
    arrive(c0)
    c0 = c_step(xh, 3)
    arrive(c1)
    c1 = c_step(other, 2)
    arrive(c0)
    c0 = c_step(xh, 4)
    arrive(c1)
    c1 = c_step(other, 3)
    arrive(a)
    a = ring4(0, "y", 2, 2)
    arrive(b)
    b = ring4(1, "x", 2, 2)
    for part in (0, 1):
        share(part, (mine[part] + 3) % 4)
        share(part, (mine[part] + 1) % 4)
    arrive(c0)
    arrive(c1)
    c1 = c_step(other, 4)
    arrive(a)
    share(0, (y + 2) % 4)
    arrive(b)
    share(1, (x + 2) % 4)
    arrive(c1)
    arrive(shared)
    links.finish()


def gather(cache, rope, weight):
    return pl.pallas_call(
        gather_kernel,
        out_shape=(
            jax.ShapeDtypeStruct((2, 8, ROWS, LAT), BF),
            jax.ShapeDtypeStruct((2, 2, 4, 4, 8, 64, HD), BF),
        ),
        in_specs=[
            pl.BlockSpec(memory_space=pltpu.VMEM),
            pl.BlockSpec(memory_space=pltpu.VMEM),
            pl.BlockSpec(memory_space=pl.ANY),
        ],
        out_specs=(pl.BlockSpec(memory_space=pl.ANY), pl.BlockSpec(memory_space=pl.ANY)),
        scratch_shapes=[
            pltpu.VMEM((ROWS, LAT), BF),
            pltpu.SemaphoreType.DMA((N_GATHER,)),
            pltpu.SemaphoreType.DMA((N_GATHER,)),
            pltpu.SemaphoreType.DMA((3,)),
        ],
        compiler_params=pltpu.CompilerParams(collective_id=0, has_side_effects=True),
        name="gather",
    )(cache, rope, weight)


def reduce_kernel(dc, d, cg_ref, rg_ref, wg_ref, *scratch):
    (acc_c, cin, xin, xout, acc_w, core_in, p1, p2, q1, q2, zin, send, recv, lsem) = scratch
    x, y, z, core, xh = place()
    other = 1 - xh
    links = Links(send, recv)
    links.barrier()
    mine = (y, x)
    local_c = [pltpu.make_async_copy(dc.at[h], acc_c.at[h], lsem.at[i]) for i, h in enumerate((other, xh))]
    for copy in local_c:
        copy.start()
    order = (2, 1, 3, 0)
    local_w, swap = {}, {}
    for k in order:
        for part in (0, 1):
            o = (mine[part] + k) % 4
            swap[part, k] = links.push(d.at[part, 1 - core, o], core_in.at[part, o], "core")
            local_w[part, k] = pltpu.make_async_copy(
                d.at[part, core, o], acc_w.at[part, o], lsem.at[2 + 4 * part + k]
            )
            local_w[part, k].start()

    def add(dst, *srcs):
        total = dst[...].astype(F32)
        for src in srcs:
            total = total + src[...].astype(F32)
        dst[...] = total.astype(BF)

    def c_send(i, hf, s):
        out = []
        for side, sign in ((0, 1), (1, -1)):
            ref = acc_c.at[hf, (z + sign * (5 - s) + 8) % 8]
            dst = cin.at[i, side, s - 1]
            if s == 1:
                rows = pl.ds(HALF * side, HALF)
                ref, dst = ref.at[rows], dst.at[rows]
            out.append(links.push(ref, dst, "z", side))
        return out

    def c_add(i, hf, s):
        for side, sign in ((0, 1), (1, -1)):
            ref = acc_c.at[hf, (z + sign * (4 - s) + 8) % 8]
            src = cin.at[i, side, s - 1]
            if s == 1:
                rows = pl.ds(HALF * side, HALF)
                ref, src = ref.at[rows], src.at[rows]
            add(ref, src)

    def core_add(k):
        for part in (0, 1):
            local_w[part, k].wait()
            swap[part, k].wait_recv()
            o = (mine[part] + k) % 4

            @pl.loop(0, 4)
            def _(i):
                add(acc_w.at[part, o, i], core_in.at[part, o, i])

    def p_send1():
        out = []
        for part, way in ((0, "y"), (1, "x")):
            o = (mine[part] + 2) % 4
            for side in (0, 1):
                rows = pl.ds(2 * side, 2)
                out.append(links.push(acc_w.at[part, o, rows], p1.at[part, side], way, side))
        return out

    def p_add1():
        for part in (0, 1):
            for side, sign in ((0, 1), (1, -1)):
                o = (mine[part] + sign + 4) % 4
                add(acc_w.at[part, o, pl.ds(2 * side, 2)], p1.at[part, side])

    def p_send2():
        out = []
        for part, way in ((0, "y"), (1, "x")):
            for side, sign in ((0, 1), (1, -1)):
                o = (mine[part] + sign + 4) % 4
                out.append(links.push(acc_w.at[part, o], p2.at[part, side], way, side))
        return out

    def p_add2():
        for part in (0, 1):

            @pl.loop(0, 4)
            def _(i):
                add(acc_w.at[part, mine[part], i], p2.at[part, 0, i], p2.at[part, 1, i])

    def q_send1():
        out = []
        for part, way in ((0, "x"), (1, "y")):
            o = (mine[1 - part] + 2) % 4
            for side in (0, 1):
                rows = pl.ds(4 * side, 4)
                out.append(links.push(acc_w.at[part, mine[part], o, rows], q1.at[part, side], way, side))
        return out

    def q_add1():
        for part in (0, 1):
            for side, sign in ((0, 1), (1, -1)):
                o = (mine[1 - part] + sign + 4) % 4
                add(acc_w.at[part, mine[part], o, pl.ds(4 * side, 4)], q1.at[part, side])

    def q_send2():
        out = []
        for part, way in ((0, "x"), (1, "y")):
            for side, sign in ((0, 1), (1, -1)):
                o = (mine[1 - part] + sign + 4) % 4
                out.append(links.push(acc_w.at[part, mine[part], o], q2.at[part, side], way, side))
        return out

    def q_add2():
        for part in (0, 1):
            add(acc_w.at[part, mine[part], mine[1 - part]], q2.at[part, 0], q2.at[part, 1])

    def z_ref(part, zo):
        return acc_w.at[part, mine[part], mine[1 - part], zo]

    def z_send(s):
        out = []
        for part in (0, 1):
            for side, sign in ((0, 1), (1, -1)):
                ref = z_ref(part, (z + sign * (5 - s) + 8) % 8)
                dst = zin.at[part, side, s - 1]
                if s == 1:
                    rows = pl.ds(32 * side, 32)
                    ref, dst = ref.at[rows], dst.at[rows]
                out.append(links.push(ref, dst, "z", side))
        return out

    def z_add(s):
        for part in (0, 1):
            for side, sign in ((0, 1), (1, -1)):
                ref = z_ref(part, (z + sign * (4 - s) + 8) % 8)
                src = zin.at[part, side, s - 1]
                if s == 1:
                    rows = pl.ds(32 * side, 32)
                    ref, src = ref.at[rows], src.at[rows]
                add(ref, src)

    for copy in local_c:
        copy.wait()
    c1 = c_send(0, other, 1)
    c0 = c_send(1, xh, 1)
    core_add(2)
    w = p_send1()
    core_add(1)
    core_add(3)
    arrive(c1)
    c_add(0, other, 1)
    c1 = c_send(0, other, 2)
    arrive(c0)
    c_add(1, xh, 1)
    c0 = c_send(1, xh, 2)
    arrive(w)
    p_add1()
    w = p_send2()
    core_add(0)
    arrive(c1)
    c_add(0, other, 2)
    c1 = c_send(0, other, 3)
    arrive(c0)
    c_add(1, xh, 2)
    c0 = c_send(1, xh, 3)
    arrive(w)
    p_add2()
    w = q_send1()
    arrive(c1)
    c_add(0, other, 3)
    c1 = c_send(0, other, 4)
    arrive(w)
    q_add1()
    w = q_send2()
    arrive(c0)
    c_add(1, xh, 3)
    arrive(w)
    q_add2()
    w = z_send(1)
    arrive(c1)
    total = acc_c[other, z].astype(F32) + cin[0, 0, 3].astype(F32) + cin[0, 1, 3].astype(F32)
    xout[...] = total.astype(BF)
    cross = links.push(xout, xin, "far")
    c0 = c_send(1, xh, 4)
    for s in (1, 2, 3):
        arrive(w)
        z_add(s)
        w = z_send(s + 1)
    arrive(w)
    for part in (0, 1):
        total = z_ref(part, z)[...].astype(F32)
        for side in (0, 1):
            total = total + zin[part, side, 3].astype(F32)
        wg_ref[part] = total
    arrive([cross])
    arrive(c0)
    total = acc_c[xh, z].astype(F32) + cin[1, 0, 3].astype(F32) + cin[1, 1, 3].astype(F32)
    total = (total + xin[...].astype(F32)).astype(BF)
    cg_ref[...] = total[0:192]
    for i in range(6):
        rg_ref[32 * i : 32 * i + 32, :] = total[192:224, 64 * i : 64 * i + 64]
    links.finish()


def reduce(dc, d):
    half = (2, 4, 4, 8, 64, HD)
    return pl.pallas_call(
        reduce_kernel,
        out_shape=(
            jax.ShapeDtypeStruct((192, LAT), BF),
            jax.ShapeDtypeStruct((192, ROPE), BF),
            jax.ShapeDtypeStruct((2, 64, HD), F32),
        ),
        in_specs=[pl.BlockSpec(memory_space=pl.ANY)] * 2,
        out_specs=(pl.BlockSpec(memory_space=pltpu.VMEM),) * 3,
        scratch_shapes=[
            pltpu.VMEM((2, 8, ROWS, LAT), BF),
            pltpu.VMEM((2, 2, 4, ROWS, LAT), BF),
            pltpu.VMEM((ROWS, LAT), BF),
            pltpu.VMEM((ROWS, LAT), BF),
            pltpu.VMEM(half, BF),
            pltpu.VMEM(half, BF),
            pltpu.VMEM((2, 2, 2, 8, 64, HD), BF),
            pltpu.VMEM((2, 2, 4, 8, 64, HD), BF),
            pltpu.VMEM((2, 2, 4, 64, HD), BF),
            pltpu.VMEM((2, 2, 8, 64, HD), BF),
            pltpu.VMEM((2, 2, 4, 64, HD), BF),
            pltpu.SemaphoreType.DMA((N_REDUCE,)),
            pltpu.SemaphoreType.DMA((N_REDUCE,)),
            pltpu.SemaphoreType.DMA((10,)),
        ],
        compiler_params=pltpu.CompilerParams(
            collective_id=1, has_side_effects=True, vmem_limit_bytes=40 * 2**20
        ),
        name="reduce",
    )(dc, d)


NT = (((1,), (1,)), ((), ()))
NN = (((1,), (0,)), ((), ()))


def dot(a, b, dims):
    return lax.dot_general(a, b, dims, preferred_element_type=F32)


def attend_kernel(ids, counts, q, qr, og, kc, w, dc, d, k, kt, rpk, r, bias, dk, dr, dense, sem):
    step = pl.program_id(0)
    xh = step % 2

    @pl.when(step == 0)
    def _():
        copies = []
        for b in range(2):
            for j in range(SEL):
                block = ids[b, j]
                owner, part = block // 3, block % 3
                rows = pl.ds(pl.multiple_of(part * 64, 64), 64)
                lanes = pl.ds(pl.multiple_of(part * 128, 128), 128)
                n = 2 * (b * SEL + j)
                copies.append(
                    pltpu.make_async_copy(kc.at[owner, rows], k.at[b, pl.ds(64 * j, 64)], sem.at[n])
                )
                copies.append(
                    pltpu.make_async_copy(kc.at[owner, pl.ds(192, 32), lanes], rpk.at[b, j], sem.at[n + 1])
                )
        for copy in copies:
            copy.start()
        row = lax.broadcasted_iota(jnp.int32, (256, 256), 0)
        col = lax.broadcasted_iota(jnp.int32, (256, 256), 1)
        for b in range(2):
            slot = row // 64
            causal = jnp.where(row % 64 <= col % 64, 0.0, -1e30).astype(F32)
            listed = jnp.where(slot < counts[b], 0.0, -1e30).astype(F32)
            bias[b] = jnp.where(slot == 0, causal, listed)
        dk[...] = jnp.zeros_like(dk)
        dr[...] = jnp.zeros_like(dr)
        for copy in copies:
            copy.wait()
        for b in range(2):
            kt[b] = k[b].T
            for j in range(SEL):
                r[b, 64 * j : 64 * j + 32, :] = rpk[b, j, :, 0:64]
                r[b, 64 * j + 32 : 64 * j + 64, :] = rpk[b, j, :, 64:128]

    spots = [(x_lo, y, core) for x_lo in range(2) for y in range(4) for core in range(2)]

    def at(part, x_lo, y, core):
        xx = 2 * xh + x_lo
        return (0, core, y, xx, 0) if part == 0 else (1, core, xx, y, 0)

    columns = []
    for head in range(4):
        part, low = head // 2, 32 * (head % 2)
        columns.append(
            jnp.concatenate([w[at(part, *spot) + (slice(low, low + 32),)] for spot in spots], axis=0)
        )
    weight = jnp.concatenate(columns, axis=1)
    dw = None
    for b in range(2):
        rows = slice(64 * b, 64 * b + 64)
        qs = jnp.concatenate([q[rows, LAT * h : LAT * h + LAT] for h in range(4)], axis=0)
        qrs = jnp.concatenate([qr[rows, ROPE * h : ROPE * h + ROPE] for h in range(4)], axis=0)
        zero = jnp.zeros((64, HD), BF)
        gd = jnp.concatenate(
            [
                jnp.concatenate(
                    [og[rows, HD * h : HD * h + HD] if i == h else zero for i in range(4)], axis=1
                )
                for h in range(4)
            ],
            axis=0,
        )
        keys = k[b]
        s = (dot(keys, qs, NT) + dot(r[b], qrs, NT)) * SCALE + bias[b]
        e = jnp.exp(s - jnp.max(s, axis=0, keepdims=True))
        prob = e * (1.0 / jnp.sum(e, axis=0, keepdims=True))
        half = prob.astype(BF)
        out_t = dot(kt[b], half, NN).astype(BF)
        part_w = dot(out_t, gd, NN)
        dw = part_w if dw is None else dw + part_w
        back = dot(gd, weight, NT).astype(BF)
        dp = dot(keys, back, NT)
        delta = jnp.sum(prob * dp, axis=0, keepdims=True)
        ds = (prob * (dp - delta)).astype(BF)
        dk[b] += dot(half, back, NN) + SCALE * dot(ds, qs, NN)
        dr[b] += dot(ds, qrs, NN)
    dw = dw.astype(BF)
    for head in range(4):
        part, low = head // 2, 32 * (head % 2)
        for i, spot in enumerate(spots):
            d[at(part, *spot) + (slice(low, low + 32),)] = dw[32 * i : 32 * i + 32, HD * head : HD * head + HD]

    @pl.when(step == pl.num_programs(0) - 1)
    def _():
        dense[...] = jnp.zeros_like(dense)
        for b in range(2):
            for j in range(SEL):
                block = ids[b, j]
                owner, part = block // 3, block % 3
                rows = pl.ds(pl.multiple_of(part * 64, 64), 64)
                dense[owner, rows, :] += dk[b, 64 * j : 64 * j + 64, :]
                lanes = pl.ds(pl.multiple_of(part * 128, 128), 128)
                low = dr[b, 64 * j : 64 * j + 32, :]
                high = dr[b, 64 * j + 32 : 64 * j + 64, :]
                dense[owner, 192:224, lanes] += SCALE * jnp.concatenate([low, high], axis=1)
        dc[...] = dense[...].astype(BF)


def attend(ids, counts, q, qr, og, kc, g):
    def group(i):
        return (i % 2) * 8 + i // 2

    gshape = (2, 2, 4, 4, 8, 64, HD)
    gblock = (2, 2, 4, 4, 1, 64, HD)
    return pl.pallas_call(
        attend_kernel,
        grid_spec=pltpu.PrefetchScalarGridSpec(
            num_scalar_prefetch=2,
            grid=(16,),
            in_specs=[
                pl.BlockSpec((128, 4 * LAT), lambda i, *_: (0, group(i))),
                pl.BlockSpec((128, 4 * ROPE), lambda i, *_: (0, group(i))),
                pl.BlockSpec((128, 4 * HD), lambda i, *_: (0, group(i))),
                pl.BlockSpec(memory_space=pl.ANY),
                pl.BlockSpec(gblock, lambda i, *_: (0, 0, 0, 0, i // 2, 0, 0)),
            ],
            out_specs=(
                pl.BlockSpec((16, ROWS, LAT), lambda i, *_: (0, 0, 0)),
                pl.BlockSpec(gblock, lambda i, *_: (0, 0, 0, 0, i // 2, 0, 0)),
            ),
            scratch_shapes=[
                pltpu.VMEM((2, 256, LAT), BF),
                pltpu.VMEM((2, LAT, 256), BF),
                pltpu.VMEM((2, SEL, 32, 128), BF),
                pltpu.VMEM((2, 256, ROPE), BF),
                pltpu.VMEM((2, 256, 256), F32),
                pltpu.VMEM((2, 256, LAT), F32),
                pltpu.VMEM((2, 256, ROPE), F32),
                pltpu.VMEM((16, ROWS, LAT), F32),
                pltpu.SemaphoreType.DMA((16,)),
            ],
        ),
        out_shape=(
            jax.ShapeDtypeStruct((16, ROWS, LAT), BF),
            jax.ShapeDtypeStruct(gshape, BF),
        ),
        compiler_params=pltpu.CompilerParams(vmem_limit_bytes=48 * 2**20),
        name="attend",
    )(ids, counts, q, qr, og, kc, g)


def shards(
    q_latent,
    q_rope,
    latent_cache,
    rope_keys,
    up_weight,
    out_grad,
    block_ids,
    block_counts,
    slab_offset,
):
    kc, g = gather(latent_cache[0], rope_keys[0], up_weight.reshape(2, 64, HD))
    dc, d = attend(
        block_ids[0],
        block_counts[0],
        q_latent[0],
        q_rope[0],
        out_grad[0],
        kc.reshape(16, ROWS, LAT),
        g,
    )
    cg, rg, wg = reduce(dc.reshape(2, 8, ROWS, LAT), d)
    return cg[None], rg[None], wg.reshape(4, 32, HD)


def solution(mesh):
    placed = (
        P("dp", "ctx", None),
        P("dp", "ctx", None),
        P("dp", "ctx", None),
        P("dp", "ctx", None),
        P("ctx", "dp", None),
        P("dp", "ctx", None),
        P("dp", "ctx", None),
        P("dp", "ctx"),
        P("dp"),
    )
    return jax.shard_map(
        shards,
        mesh=mesh,
        in_specs=placed,
        out_specs=(P("dp", "ctx", None), P("dp", "ctx", None), P("ctx", "dp", None)),
        check_vma=False,
    )
```

```python
import functools

import jax
import jax.numpy as jnp
from jax import lax
from jax.experimental import pallas as pl
from jax.experimental.pallas import tpu as pltpu
from jax.sharding import PartitionSpec as P

LAT = 512
ROPE = 64
HD = 128
BLK = 64
SEL = 4
SCALE = (HD + ROPE) ** (-0.5)
TILES = 14
HALF = TILES // 2
MESH = pl.DeviceIdType.MESH
BF = jnp.bfloat16
F32 = jnp.float32


def place():
    dp, ctx = lax.axis_index("dp"), lax.axis_index("ctx")
    core, y, x_lo = dp % 2, (dp // 2) % 4, dp // 8
    x_hi, z = ctx // 8, ctx % 8
    return x_hi * 2 + x_lo, y, z, core, x_hi


def device(x, y, z, core):
    return (((x % 2) * 4 + y) * 2 + core, (x // 2) * 8 + z)


class Links:
    def __init__(self, send, recv):
        x, y, z, core, _ = place()
        self.send, self.recv, self.count, self.started = send, recv, 0, []
        self.to = {
            "z": (device(x, y, (z + 1) % 8, core), device(x, y, (z + 7) % 8, core)),
            "y": (device(x, (y + 1) % 4, z, core), device(x, (y + 3) % 4, z, core)),
            "x": (device((x + 1) % 4, y, z, core), device((x + 3) % 4, y, z, core)),
            "far": (device((x + 2) % 4, y, z, core),),
            "core": (device(x, y, z, 1 - core),),
        }
        for n in range(1, 8):
            self.to["z", n] = (device(x, y, (z + n) % 8, core),)

    def barrier(self):
        sem = pltpu.get_barrier_semaphore()
        partners = [d for way, group in self.to.items() if way != "z" for d in group]
        for d in partners:
            pl.semaphore_signal(sem, inc=1, device_id=d, device_id_type=MESH)
        pl.semaphore_wait(sem, len(partners))

    def push(self, src, dst, way, side=0, start=True):
        i = self.count
        self.count += 1
        copy = pltpu.make_async_remote_copy(
            src_ref=src,
            dst_ref=dst,
            send_sem=self.send.at[i],
            recv_sem=self.recv.at[i],
            device_id=self.to[way][side],
            device_id_type=MESH,
        )
        if start:
            copy.start()
        self.started.append(copy)
        return copy

    def finish(self):
        for copy in self.started:
            copy.wait_send()


def arrive(copies):
    for copy in copies:
        copy.wait_recv()


NT = (((1,), (1,)), ((), ()))
NN = (((1,), (0,)), ((), ()))


def dot(a, b, dims):
    return lax.dot_general(a, b, dims, preferred_element_type=F32)


def lanes_of(c, width):
    return pl.ds(pl.multiple_of(c * width, width), width)


SPOTS = [(x_lo, y, core) for x_lo in range(2) for y in range(4) for core in range(2)]


def weight_at(part, xh, x_lo, y, core, z):
    return (core, y, 2 * xh + x_lo, z, slice(64 * part, 64 * part + 64))


def grad_at(part, xh, x_lo, y, core, z):
    xx = 2 * xh + x_lo
    return (0, core, y, xx, z) if part == 0 else (1, core, xx, y, z)


def grads_of_pair(og, i, xh, part):
    low = og[:, lanes_of((xh * 8 + i) * 2 + part, 2 * HD)]
    zero = jnp.zeros((64, HD), BF)
    rows = []
    for b in range(2):
        first, second = low[64 * b : 64 * b + 64, :HD], low[64 * b : 64 * b + 64, HD:]
        rows.append(jnp.concatenate([first, zero], axis=1))
        rows.append(jnp.concatenate([zero, second], axis=1))
    return jnp.concatenate(rows, axis=0)


def queries(q, i, b):
    parts = []
    for xh in range(2):
        block = q[64 * b : 64 * b + 64, lanes_of(xh * 8 + i, 4 * LAT)]
        parts += [block[:, LAT * j : LAT * j + LAT] for j in range(4)]
    return jnp.concatenate(parts, axis=0)


def rotary(qr, i, b):
    low = lax.broadcasted_iota(jnp.int32, (64, 128), 1) < 64
    parts = []
    for xh in range(2):
        block = qr[64 * b : 64 * b + 64, lanes_of(xh * 8 + i, 4 * ROPE)].astype(F32)
        for j in range(4):
            slab = block[:, 128 * (j // 2) : 128 * (j // 2) + 128]
            slab = jnp.where(low, slab, 0.0) if j % 2 == 0 else jnp.where(low, 0.0, slab)
            parts.append(slab.astype(BF))
    return jnp.concatenate(parts, axis=0)


def forward(i, q, qr, og, k, kt, bias, ph, d):
    outs = []
    for b in range(2):
        qs = jnp.concatenate([queries(q, i, b), rotary(qr, i, b)], axis=1)
        s = dot(k[b], qs, NT) * SCALE + jnp.concatenate([bias[b]] * 4, axis=1)
        e = jnp.exp(s - jnp.max(s, axis=0, keepdims=True))
        half = (e * (1.0 / jnp.sum(e, axis=0, keepdims=True))).astype(BF)
        ph[i, b] = half
        outs.append(dot(kt[b], half, NN).astype(BF))
    for pair in range(4):
        xh, part = pair // 2, pair % 2
        both = jnp.concatenate([out[:, 128 * pair : 128 * pair + 128] for out in outs], axis=1)
        dw = dot(both, grads_of_pair(og, i, xh, part), NN).astype(BF)
        for n, spot in enumerate(SPOTS):
            rows = dw[32 * n : 32 * n + 32]
            d[grad_at(part, xh, *spot, i)] = jnp.concatenate([rows[:, :HD], rows[:, HD:]], axis=0)


def backward(i, q, qr, og, k, w, ph, dk, dr):
    backs = []
    for pair in range(4):
        xh, part = pair // 2, pair % 2
        pieces = [w[weight_at(part, xh, *spot, i)] for spot in SPOTS]
        weight = jnp.concatenate(
            [jnp.concatenate([p[:32], p[32:]], axis=1) for p in pieces], axis=0
        )
        backs.append(dot(grads_of_pair(og, i, xh, part), weight, NT).astype(BF))
    for b in range(2):
        back = jnp.concatenate([back[128 * b : 128 * b + 128] for back in backs], axis=0)
        dp = dot(k[b, :, :LAT], back, NT)
        half = ph[i, b]
        prob = half.astype(F32)
        weighted = prob * dp
        delta = jnp.sum(weighted, axis=0, keepdims=True)
        ds = ((weighted - prob * delta) * SCALE).astype(BF)
        dk[b] += dot(
            jnp.concatenate([half, ds], axis=1), jnp.concatenate([back, queries(q, i, b)], axis=0), NN
        )
        dr[b] += dot(ds, rotary(qr, i, b), NN)


def core_kernel(
    ids, counts, cache, rope, w_in, q_hbm, qr_hbm, og_hbm, cg, rg, wg,
    kc, g, d, core_in, q, qr, og, rope_v, k, kt, bias, ph, dk, dr, drp, cin, p1, p2, q1, q2, zin,
    send, recv, lsem,
):
    x, y, z, core, xh = place()
    links = Links(send, recv)
    mine = (y, x)

    def own(n):
        return xh * 8 + (z + n + 8) % 8

    def oth(n):
        return (1 - xh) * 8 + (z + n + 8) % 8

    def upper(side):
        return pl.ds(HALF * side, HALF)

    first = [
        pltpu.make_async_copy(cache, kc.at[own(0), pl.ds(0, 12)], lsem.at[0]),
        pltpu.make_async_copy(rope, rope_v, lsem.at[1]),
        pltpu.make_async_copy(w_in, g.at[core, y, x, z], lsem.at[2]),
    ]
    loads = [
        pltpu.make_async_copy(qr_hbm, qr, lsem.at[4]),
        pltpu.make_async_copy(og_hbm, og, lsem.at[5]),
        pltpu.make_async_copy(q_hbm, q, lsem.at[6]),
    ]
    for copy in first + loads:
        copy.start()
    links.barrier()
    for copy in first:
        copy.wait()
    flipped = jnp.concatenate([rope_v[...].astype(F32), jnp.zeros((ROPE, 64), F32)], axis=1)
    flipped = jnp.concatenate([flipped, jnp.zeros((128 - ROPE, 256), F32)], axis=0).T
    packed = [flipped[32 * i : 32 * i + 32, :ROPE].astype(BF) for i in range(6)]
    packed = jnp.concatenate(packed + [jnp.zeros((32, 128), BF)], axis=1)
    kc[own(0), 12] = packed[:16]
    kc[own(0), 13] = packed[16:]

    def ring_x(s):
        out = []
        for side, sign in ((0, 1), (1, -1)):
            if s == 1:
                ref = g.at[core, y, x]
            else:
                ref = g.at[core, y, (x - sign + 4) % 4, pl.ds(4 * side, 4)]
            out.append(links.push(ref, ref, "x", side))
        return out

    def ring_y1(n):
        ref = g.at[core, y, (x + n + 4) % 4]
        return [links.push(ref, ref, "y", side) for side in (0, 1)]

    def ring_y2(n, start=True):
        out = []
        for side, sign in ((0, 1), (1, -1)):
            ref = g.at[core, (y - sign + 4) % 4, (x + n + 4) % 4, pl.ds(4 * side, 4)]
            out.append(links.push(ref, ref, "y", side, start))
        return out

    shared = []

    def share(n, start=True):
        ref = g.at[core, (y + n) % 4]
        shared.append(links.push(ref, ref, "core", 0, start))
        return shared[-1]

    def ring8(s):
        out = []
        for side, sign in ((0, 1), (1, -1)):
            ref = kc.at[own(-sign * (s - 1))]
            if s == 4:
                ref = ref.at[upper(side)]
            out.append(links.push(ref, ref, "z", side))
        return out

    def push_block(o, way, side=0, rows=None):
        ref = kc.at[o]
        if rows is not None:
            ref = ref.at[rows]
        return links.push(ref, ref, way, side)

    weights = g.at[core, y, x, z]
    c = ring8(1)
    cross0 = push_block(own(0), "far")
    wz = [links.push(weights, weights, ("z", n)) for n in (4, 3, 5, 2, 6, 1, 7)]
    arrive(c)
    c = ring8(2)
    cross1 = [push_block(own(1), "far", 0, upper(0)), push_block(own(-1), "far", 0, upper(1))]
    arrive(wz)
    ya = ring_y1(0)
    wx = ring_x(1)
    arrive([cross0])
    near = [push_block(oth(0), "z", 0, upper(0)), push_block(oth(0), "z", 1, upper(1))]
    arrive(c)
    c = ring8(3)
    cross2 = [push_block(own(2), "far"), push_block(own(-2), "far")]
    arrive(ya)
    ya2 = ring_y2(0)
    arrive(wx)
    wx = ring_x(2)
    yb = ring_y1(1) + ring_y1(-1)
    arrive(c)
    c = ring8(4)
    arrive(c)
    cross4 = push_block(own(4), "far")
    arrive(wx)
    yc = ring_y1(2)
    share(0)
    arrive(cross2)
    third = [push_block(oth(-2), "z", 0), push_block(oth(2), "z", 1)]
    arrive(yb)
    yb2 = ring_y2(1) + ring_y2(-1)
    row = lax.broadcasted_iota(jnp.int32, (256, 128), 0)
    col = lax.broadcasted_iota(jnp.int32, (256, 128), 1)
    for n in range(2):
        slot = row // 64
        causal = jnp.where(row % 64 <= col % 64, 0.0, -1e30).astype(F32)
        listed = jnp.where(slot < counts[n], 0.0, -1e30).astype(F32)
        bias[n] = jnp.where(slot == 0, causal, listed)
    dk[...] = jnp.zeros_like(dk)
    dr[...] = jnp.zeros_like(dr)
    for copy in loads:
        copy.wait()
    arrive(cross1)
    arrive(near)
    arrive([cross4])
    arrive(third)

    for n in range(2):
        for j in range(SEL):
            owner, part = lax.div(ids[n, j], 3), lax.rem(ids[n, j], 3)
            for r in range(4):
                k[n, 64 * j + 16 * r : 64 * j + 16 * r + 16, :LAT] = kc[owner, 4 * part + r]
            for r in range(2):
                packs = kc[owner, 12 + r].astype(F32)
                pack = packs[:, 256:384]
                pack = jnp.where(part == 0, packs[:, 0:128], pack)
                pack = jnp.where(part == 1, packs[:, 128:256], pack)
                low, high = pack[:, :64].astype(BF), pack[:, 64:].astype(BF)
                row = 64 * j + 16 * r
                k[n, row : row + 16, LAT:] = jnp.concatenate([low, low], axis=1)
                k[n, row + 32 : row + 48, LAT:] = jnp.concatenate([high, high], axis=1)
        kt[n] = k[n, :, :LAT].T

    first_swap = links.count
    links.count += 8

    def swap(i):
        return pltpu.make_async_remote_copy(
            src_ref=d.at[:, 1 - core, :, :, i],
            dst_ref=core_in.at[:, :, :, i],
            send_sem=send.at[first_swap + i],
            recv_sem=recv.at[first_swap + i],
            device_id=links.to["core"][0],
            device_id_type=MESH,
        )

    def add(dst, *srcs):
        total = dst[...].astype(F32)
        for src in srcs:
            total = total + src[...].astype(F32)
        dst[...] = total.astype(BF)

    def swap_add(i):
        swap(i).wait_recv()
        for part in (0, 1):
            for n in range(4):
                add(d.at[part, core, n, :, i], core_in.at[part, n, :, i])

    def p_send1(h, start=True):
        out = []
        for part, way in ((0, "y"), (1, "x")):
            for side in (0, 1):
                ref = d.at[part, core, (mine[part] + 2) % 4, pl.ds(2 * side, 2), pl.ds(4 * h, 4)]
                out.append(links.push(ref, p1.at[h, part, side], way, side, start))
        return out

    def p_add1(h):
        for part in (0, 1):
            for side, sign in ((0, 1), (1, -1)):
                o = (mine[part] + sign + 4) % 4
                for n in range(2):
                    add(d.at[part, core, o, 2 * side + n, pl.ds(4 * h, 4)], p1.at[h, part, side, n])

    def p_send2(h, start=True):
        out = []
        for part, way in ((0, "y"), (1, "x")):
            for side, sign in ((0, 1), (1, -1)):
                ref = d.at[part, core, (mine[part] + sign + 4) % 4, :, pl.ds(4 * h, 4)]
                out.append(links.push(ref, p2.at[h, part, side], way, side, start))
        return out

    def p_add2(h):
        for part in (0, 1):
            for n in range(4):
                ref = d.at[part, core, mine[part], n, pl.ds(4 * h, 4)]
                add(ref, p2.at[h, part, 0, n], p2.at[h, part, 1, n])

    def q_send1():
        out = []
        for part, way in ((0, "x"), (1, "y")):
            o = (mine[1 - part] + 2) % 4
            for side in (0, 1):
                rows = pl.ds(4 * side, 4)
                out.append(links.push(d.at[part, core, mine[part], o, rows], q1.at[part, side], way, side))
        return out

    def q_add1():
        for part in (0, 1):
            for side, sign in ((0, 1), (1, -1)):
                o = (mine[1 - part] + sign + 4) % 4
                add(d.at[part, core, mine[part], o, pl.ds(4 * side, 4)], q1.at[part, side])

    def q_send2():
        out = []
        for part, way in ((0, "x"), (1, "y")):
            for side, sign in ((0, 1), (1, -1)):
                o = (mine[1 - part] + sign + 4) % 4
                out.append(links.push(d.at[part, core, mine[part], o], q2.at[part, side], way, side))
        return out

    def q_add2():
        for part in (0, 1):
            add(d.at[part, core, mine[part], mine[1 - part]], q2.at[part, 0], q2.at[part, 1])

    def total_of(part):
        total = d[part, core, mine[part], mine[1 - part], z].astype(F32)
        for n in range(7):
            total = total + zin[part, n].astype(F32)
        return total

    yc2 = ring_y2(2, False)
    late = [share(1, False), share(3, False), share(2, False)]
    pa1 = p_send1(0, False)

    @pl.loop(0, 8)
    def _(i):
        forward(i, q, qr, og, k, kt, bias, ph, d)
        swap(i).start()

        @pl.when(i > 0)
        def _():
            swap_add(i - 1)

        @pl.when(i == 0)
        def _():
            arrive(yc)
            for copy in yc2:
                copy.start()
            late[0].start()
            late[1].start()

        @pl.when(i == 4)
        def _():
            for copy in pa1:
                copy.start()

        @pl.when(i == 5)
        def _():
            arrive(ya2)
            arrive(yb2)
            arrive(yc2)
            late[2].start()

    swap_add(7)
    pb1 = p_send1(1)
    arrive(shared)
    pa2, pb2 = p_send2(0, False), p_send2(1, False)

    @pl.loop(0, 8)
    def _(i):
        backward(i, q, qr, og, k, g, ph, dk, dr)

        @pl.when(i == 0)
        def _():
            arrive(pa1)
            p_add1(0)
            for copy in pa2:
                copy.start()

        @pl.when(i == 2)
        def _():
            arrive(pb1)
            p_add1(1)
            for copy in pb2:
                copy.start()

        @pl.when(i == 6)
        def _():
            arrive(pa2)
            p_add2(0)

    links.finish()
    links.started = []
    for n in range(2):
        for j in range(SEL):
            fold = dr[n, 64 * j : 64 * j + 64, :]
            fold = fold[:, :64] + fold[:, 64:]
            drp[SEL * n + j] = jnp.concatenate([fold[:32], fold[32:]], axis=1)

    def fill(o):
        hits = [
            [jnp.where(ids[n, j] == o * 3 + part, 1.0, 0.0).astype(F32) for n in range(2) for j in range(SEL)]
            for part in range(3)
        ]
        packs = []
        for part in range(3):
            pack = jnp.zeros((32, 128), F32)
            for n in range(2 * SEL):
                pack = pack + hits[part][n] * drp[n]
            packs.append(pack.astype(BF))
            for r in range(4):
                total = jnp.zeros((16, LAT), F32)
                for n in range(2 * SEL):
                    low = 64 * (n % SEL) + 16 * r
                    total = total + hits[part][n] * dk[n // SEL, low : low + 16, :]
                kc[o, 4 * part + r] = total.astype(BF)
        packs = jnp.concatenate(packs + [jnp.zeros((32, 128), BF)], axis=1)
        kc[o, 12] = packs[:16]
        kc[o, 13] = packs[16:]

    def away(o, slot, way, side=0, rows=None):
        src, dst = kc.at[o], cin.at[slot]
        if rows is not None:
            src, dst = src.at[rows], dst.at[rows]
        return links.push(src, dst, way, side)

    def take(o, slots, rows=slice(None)):
        total = kc[o, rows].astype(F32)
        for slot in slots:
            total = total + cin[slot, rows].astype(F32)
        kc[o, rows] = total.astype(BF)

    lower, higher = slice(0, HALF), slice(HALF, TILES)
    fill(oth(4))
    cross4 = away(oth(4), 0, "far")
    fill(oth(3))
    fill(oth(-3))
    third = [away(oth(3), 1, "z", 0), away(oth(-3), 2, "z", 1)]
    fill(oth(2))
    fill(oth(-2))
    fill(own(4))
    arrive(pb2)
    p_add2(1)
    w = q_send1()
    arrive(third)
    take(oth(2), [1])
    take(oth(-2), [2])
    cross2 = [away(oth(2), 3, "far"), away(oth(-2), 4, "far")]
    arrive([cross4])
    take(own(4), [0])
    c = [away(own(4), 5, "z", 0, upper(0)), away(own(4), 6, "z", 1, upper(1))]
    fill(own(3))
    fill(own(-3))
    arrive(w)
    q_add1()
    w = q_send2()
    arrive(c)
    take(own(3), [5], lower)
    take(own(-3), [6], higher)
    c = [away(own(3), 7, "z", 0), away(own(-3), 8, "z", 1)]
    fill(oth(1))
    fill(oth(-1))
    near = [away(oth(1), 9, "z", 0, upper(1)), away(oth(-1), 10, "z", 1, upper(0))]
    cross1 = [away(oth(1), 11, "far", 0, upper(0)), away(oth(-1), 12, "far", 0, upper(1))]
    fill(own(2))
    fill(own(-2))
    fill(oth(0))
    arrive(w)
    q_add2()
    w = [
        links.push(
            d.at[part, core, mine[part], mine[1 - part], (z + n) % 8], zin.at[part, n - 1], ("z", n)
        )
        for n in (4, 3, 5, 2, 6, 1, 7)
        for part in (0, 1)
    ]
    arrive(c)
    arrive(cross2)
    take(own(2), [7, 3])
    take(own(-2), [8, 4])
    c = [away(own(2), 13, "z", 0), away(own(-2), 14, "z", 1)]
    arrive(near)
    take(oth(0), [9], higher)
    take(oth(0), [10], lower)
    cross0 = away(oth(0), 15, "far")
    fill(own(1))
    fill(own(-1))
    fill(own(0))
    arrive(cross1)
    take(own(1), [11], lower)
    take(own(-1), [12], higher)
    arrive(c)
    take(own(1), [13])
    take(own(-1), [14])
    c = [away(own(1), 16, "z", 0), away(own(-1), 17, "z", 1)]
    arrive(w)
    wg[0:64, :] = total_of(0)
    wg[64:128, :] = total_of(1)
    arrive([cross0])
    arrive(c)
    total = kc[own(0)].astype(F32)
    for slot in (15, 16, 17):
        total = total + cin[slot].astype(F32)
    cg[...] = total[0:12].astype(BF)
    pack = total[12:14].reshape(32, LAT)
    rows = [pack[:, 64 * i : 64 * i + 64] for i in range(6)] + [jnp.zeros((64, ROPE), F32)]
    flipped = jnp.concatenate(rows, axis=0)
    flipped = jnp.concatenate([flipped, jnp.zeros((256, 128 - ROPE), F32)], axis=1).T
    rg[...] = flipped[:ROPE, :192].astype(BF)
    links.finish()

    @pl.loop(0, 8)
    def _(i):
        swap(i).wait_send()


def run(ids, counts, cache, rope, weight, q, qr, og):
    return pl.pallas_call(
        core_kernel,
        out_shape=(
            jax.ShapeDtypeStruct((12, 16, LAT), BF),
            jax.ShapeDtypeStruct((ROPE, 192), BF),
            jax.ShapeDtypeStruct((128, HD), F32),
        ),
        in_specs=[pl.BlockSpec(memory_space=pltpu.SMEM)] * 2 + [pl.BlockSpec(memory_space=pl.ANY)] * 6,
        out_specs=(pl.BlockSpec(memory_space=pltpu.VMEM),) * 3,
        scratch_shapes=[
            pltpu.VMEM((16, TILES, 16, LAT), BF),
            pltpu.VMEM((2, 4, 4, 8, 128, HD), BF),
            pltpu.VMEM((2, 2, 4, 4, 8, 64, HD), BF),
            pltpu.VMEM((2, 4, 4, 8, 64, HD), BF),
            pltpu.VMEM((128, 64 * LAT), BF),
            pltpu.VMEM((128, 64 * ROPE), BF),
            pltpu.VMEM((128, 64 * HD), BF),
            pltpu.VMEM((ROPE, 192), BF),
            pltpu.VMEM((2, 256, LAT + 128), BF),
            pltpu.VMEM((2, LAT, 256), BF),
            pltpu.VMEM((2, 256, 128), F32),
            pltpu.VMEM((8, 2, 256, 512), BF),
            pltpu.VMEM((2, 256, LAT), F32),
            pltpu.VMEM((2, 256, 128), F32),
            pltpu.VMEM((2 * SEL, 32, 128), F32),
            pltpu.VMEM((18, TILES, 16, LAT), BF),
            pltpu.VMEM((2, 2, 2, 2, 4, 64, HD), BF),
            pltpu.VMEM((2, 2, 2, 4, 4, 64, HD), BF),
            pltpu.VMEM((2, 2, 4, 64, HD), BF),
            pltpu.VMEM((2, 2, 8, 64, HD), BF),
            pltpu.VMEM((2, 7, 64, HD), BF),
            pltpu.SemaphoreType.DMA((130,)),
            pltpu.SemaphoreType.DMA((130,)),
            pltpu.SemaphoreType.DMA((7,)),
        ],
        compiler_params=pltpu.CompilerParams(
            collective_id=0, has_side_effects=True, vmem_limit_bytes=63 * 2**20
        ),
        name="whole",
    )(ids, counts, cache, rope, weight, q, qr, og)


def shards(
    q_latent,
    q_rope,
    latent_cache,
    rope_keys,
    up_weight,
    out_grad,
    block_ids,
    block_counts,
    slab_offset,
):
    cg, rg, wg = run(
        block_ids[0],
        block_counts[0],
        latent_cache.reshape(12, 16, LAT),
        rope_keys[0].T,
        up_weight.reshape(128, HD),
        q_latent[0],
        q_rope[0],
        out_grad[0],
    )
    return cg.reshape(1, 192, LAT), rg.T[None], wg.reshape(4, 32, HD)


def solution(mesh):
    placed = (
        P("dp", "ctx", None),
        P("dp", "ctx", None),
        P("dp", "ctx", None),
        P("dp", "ctx", None),
        P("ctx", "dp", None),
        P("dp", "ctx", None),
        P("dp", "ctx", None),
        P("dp", "ctx"),
        P("dp"),
    )
    return jax.shard_map(
        shards,
        mesh=mesh,
        in_specs=placed,
        out_specs=(P("dp", "ctx", None), P("dp", "ctx", None), P("ctx", "dp", None)),
        check_vma=False,
    )
```

```python
import functools

import jax
import jax.numpy as jnp
from jax import lax
from jax.experimental import pallas as pl
from jax.experimental.pallas import tpu as pltpu
from jax.sharding import PartitionSpec as P

LAT = 512
ROPE = 64
HD = 128
BLK = 64
SEL = 4
SCALE = (HD + ROPE) ** (-0.5)
TILES = 14
HALF = TILES // 2
MESH = pl.DeviceIdType.MESH
BF = jnp.bfloat16
F32 = jnp.float32


def place():
    dp, ctx = lax.axis_index("dp"), lax.axis_index("ctx")
    core, y, x_lo = dp % 2, (dp // 2) % 4, dp // 8
    x_hi, z = ctx // 8, ctx % 8
    return x_hi * 2 + x_lo, y, z, core, x_hi


def device(x, y, z, core):
    return (((x % 2) * 4 + y) * 2 + core, (x // 2) * 8 + z)


class Links:
    def __init__(self, send, recv):
        x, y, z, core, _ = place()
        self.send, self.recv, self.count, self.started = send, recv, 0, []
        self.to = {
            "z": (device(x, y, (z + 1) % 8, core), device(x, y, (z + 7) % 8, core)),
            "y": (device(x, (y + 1) % 4, z, core), device(x, (y + 3) % 4, z, core)),
            "x": (device((x + 1) % 4, y, z, core), device((x + 3) % 4, y, z, core)),
            "far": (device((x + 2) % 4, y, z, core),),
            "core": (device(x, y, z, 1 - core),),
        }
        for n in range(1, 8):
            self.to["z", n] = (device(x, y, (z + n) % 8, core),)

    def barrier(self):
        sem = pltpu.get_barrier_semaphore()
        partners = [d for way, group in self.to.items() if way != "z" for d in group]
        for d in partners:
            pl.semaphore_signal(sem, inc=1, device_id=d, device_id_type=MESH)
        pl.semaphore_wait(sem, len(partners))

    def push(self, src, dst, way, side=0, start=True):
        i = self.count
        self.count += 1
        copy = pltpu.make_async_remote_copy(
            src_ref=src,
            dst_ref=dst,
            send_sem=self.send.at[i],
            recv_sem=self.recv.at[i],
            device_id=self.to[way][side],
            device_id_type=MESH,
        )
        if start:
            copy.start()
        self.started.append(copy)
        return copy

    def finish(self):
        for copy in self.started:
            copy.wait_send()


def arrive(copies):
    for copy in copies:
        copy.wait_recv()


NT = (((1,), (1,)), ((), ()))
NN = (((1,), (0,)), ((), ()))


def dot(a, b, dims):
    return lax.dot_general(a, b, dims, preferred_element_type=F32)


def lanes_of(c, width):
    return pl.ds(pl.multiple_of(c * width, width), width)


SPOTS = [(x_lo, y, core) for x_lo in range(2) for y in range(4) for core in range(2)]


def weight_at(part, xh, x_lo, y, core, z):
    return (core, y, 2 * xh + x_lo, z, slice(64 * part, 64 * part + 64))


def grad_at(part, xh, x_lo, y, core, z):
    xx = 2 * xh + x_lo
    return (0, core, y, xx, z) if part == 0 else (1, core, xx, y, z)


def grads_of_pair(og, i, xh, part):
    low = og[:, lanes_of((xh * 8 + i) * 2 + part, 2 * HD)]
    zero = jnp.zeros((64, HD), BF)
    rows = []
    for b in range(2):
        first, second = low[64 * b : 64 * b + 64, :HD], low[64 * b : 64 * b + 64, HD:]
        rows.append(jnp.concatenate([first, zero], axis=1))
        rows.append(jnp.concatenate([zero, second], axis=1))
    return jnp.concatenate(rows, axis=0)


def queries(q, i, b):
    parts = []
    for xh in range(2):
        block = q[64 * b : 64 * b + 64, lanes_of(xh * 8 + i, 4 * LAT)]
        parts += [block[:, LAT * j : LAT * j + LAT] for j in range(4)]
    return jnp.concatenate(parts, axis=0)


def rotary(qr, i, b):
    low = lax.broadcasted_iota(jnp.int32, (64, 128), 1) < 64
    parts = []
    for xh in range(2):
        block = qr[64 * b : 64 * b + 64, lanes_of(xh * 8 + i, 4 * ROPE)].astype(F32)
        for j in range(4):
            slab = block[:, 128 * (j // 2) : 128 * (j // 2) + 128]
            slab = jnp.where(low, slab, 0.0) if j % 2 == 0 else jnp.where(low, 0.0, slab)
            parts.append(slab.astype(BF))
    return jnp.concatenate(parts, axis=0)


def forward(i, q, qr, og, k, kt, bias, ph, d):
    outs = []
    for b in range(2):
        qs = jnp.concatenate([queries(q, i, b), rotary(qr, i, b)], axis=1)
        s = dot(k[b], qs, NT) * SCALE + jnp.concatenate([bias[b]] * 4, axis=1)
        e = jnp.exp(s - jnp.max(s, axis=0, keepdims=True))
        half = (e * (1.0 / jnp.sum(e, axis=0, keepdims=True))).astype(BF)
        ph[i, b] = half
        outs.append(dot(kt[b], half, NN).astype(BF))
    for pair in range(4):
        xh, part = pair // 2, pair % 2
        both = jnp.concatenate([out[:, 128 * pair : 128 * pair + 128] for out in outs], axis=1)
        dw = dot(both, grads_of_pair(og, i, xh, part), NN).astype(BF)
        for n, spot in enumerate(SPOTS):
            rows = dw[32 * n : 32 * n + 32]
            d[grad_at(part, xh, *spot, i)] = jnp.concatenate([rows[:, :HD], rows[:, HD:]], axis=0)


def backward(i, q, qr, og, k, w, ph, dk, dr):
    backs = []
    for pair in range(4):
        xh, part = pair // 2, pair % 2
        pieces = [w[weight_at(part, xh, *spot, i)] for spot in SPOTS]
        weight = jnp.concatenate(
            [jnp.concatenate([p[:32], p[32:]], axis=1) for p in pieces], axis=0
        )
        backs.append(dot(grads_of_pair(og, i, xh, part), weight, NT).astype(BF))
    for b in range(2):
        back = jnp.concatenate([back[128 * b : 128 * b + 128] for back in backs], axis=0)
        dp = dot(k[b, :, :LAT], back, NT)
        half = ph[i, b]
        prob = half.astype(F32)
        weighted = prob * dp
        delta = jnp.sum(weighted, axis=0, keepdims=True)
        ds = ((weighted - prob * delta) * SCALE).astype(BF)
        dk[b] += dot(
            jnp.concatenate([half, ds], axis=1), jnp.concatenate([back, queries(q, i, b)], axis=0), NN
        )
        dr[b] += dot(ds, rotary(qr, i, b), NN)


def core_kernel(
    ids, counts, cache, rope, w_in, q_hbm, qr_hbm, og_hbm, cg, rg, wg,
    kc, g, d, core_in, q, qr, og, rope_v, k, kt, bias, ph, dk, dr, drp, cin, p1, p2, q1, q2, zin,
    send, recv, lsem,
):
    x, y, z, core, xh = place()
    links = Links(send, recv)
    mine = (y, x)

    def own(n):
        return xh * 8 + (z + n + 8) % 8

    def oth(n):
        return (1 - xh) * 8 + (z + n + 8) % 8

    def upper(side):
        return pl.ds(HALF * side, HALF)

    first = [
        pltpu.make_async_copy(cache, kc.at[own(0), pl.ds(0, 12)], lsem.at[0]),
        pltpu.make_async_copy(rope, rope_v, lsem.at[1]),
        pltpu.make_async_copy(w_in, g.at[core, y, x, z], lsem.at[2]),
    ]
    loads = [
        pltpu.make_async_copy(qr_hbm, qr, lsem.at[4]),
        pltpu.make_async_copy(og_hbm, og, lsem.at[5]),
        pltpu.make_async_copy(q_hbm, q, lsem.at[6]),
    ]
    for copy in first + loads:
        copy.start()
    links.barrier()
    for copy in first:
        copy.wait()
    flipped = jnp.concatenate([rope_v[...].astype(F32), jnp.zeros((ROPE, 64), F32)], axis=1)
    flipped = jnp.concatenate([flipped, jnp.zeros((128 - ROPE, 256), F32)], axis=0).T
    packed = [flipped[32 * i : 32 * i + 32, :ROPE].astype(BF) for i in range(6)]
    packed = jnp.concatenate(packed + [jnp.zeros((32, 128), BF)], axis=1)
    kc[own(0), 12] = packed[:16]
    kc[own(0), 13] = packed[16:]

    def ring_x(s):
        out = []
        for side, sign in ((0, 1), (1, -1)):
            if s == 1:
                ref = g.at[core, y, x]
            else:
                ref = g.at[core, y, (x - sign + 4) % 4, pl.ds(4 * side, 4)]
            out.append(links.push(ref, ref, "x", side))
        return out

    def ring_y1(n):
        ref = g.at[core, y, (x + n + 4) % 4]
        return [links.push(ref, ref, "y", side) for side in (0, 1)]

    def ring_y2(n, start=True):
        out = []
        for side, sign in ((0, 1), (1, -1)):
            ref = g.at[core, (y - sign + 4) % 4, (x + n + 4) % 4, pl.ds(4 * side, 4)]
            out.append(links.push(ref, ref, "y", side, start))
        return out

    shared = []

    def share(n, start=True):
        ref = g.at[core, (y + n) % 4]
        shared.append(links.push(ref, ref, "core", 0, start))
        return shared[-1]

    def ring8(s):
        out = []
        for side, sign in ((0, 1), (1, -1)):
            ref = kc.at[own(-sign * (s - 1))]
            if s == 4:
                ref = ref.at[upper(side)]
            out.append(links.push(ref, ref, "z", side))
        return out

    def push_block(o, way, side=0, rows=None):
        ref = kc.at[o]
        if rows is not None:
            ref = ref.at[rows]
        return links.push(ref, ref, way, side)

    weights = g.at[core, y, x, z]
    c = ring8(1)
    cross0 = push_block(own(0), "far")
    wz = [links.push(weights, weights, ("z", n)) for n in (4, 3, 5, 2, 6, 1, 7)]
    arrive(c)
    c = ring8(2)
    arrive(wz)
    ya = ring_y1(0)
    wx = ring_x(1)
    arrive([cross0])
    near = [push_block(oth(0), "z", 0), push_block(oth(0), "z", 1)]
    arrive(c)
    c = ring8(3)
    cross2 = [push_block(own(2), "far"), push_block(own(-2), "far")]
    arrive(ya)
    ya2 = ring_y2(0)
    arrive(wx)
    wx = ring_x(2)
    yb = ring_y1(1) + ring_y1(-1)
    arrive(c)
    c = ring8(4)
    arrive(c)
    cross4 = push_block(own(4), "far")
    arrive(wx)
    yc = ring_y1(2)
    share(0)
    arrive(cross2)
    third = [push_block(oth(-2), "z", 0), push_block(oth(2), "z", 1)]
    arrive(yb)
    yb2 = ring_y2(1) + ring_y2(-1)
    row = lax.broadcasted_iota(jnp.int32, (256, 128), 0)
    col = lax.broadcasted_iota(jnp.int32, (256, 128), 1)
    for n in range(2):
        slot = row // 64
        causal = jnp.where(row % 64 <= col % 64, 0.0, -1e30).astype(F32)
        listed = jnp.where(slot < counts[n], 0.0, -1e30).astype(F32)
        bias[n] = jnp.where(slot == 0, causal, listed)
    dk[...] = jnp.zeros_like(dk)
    dr[...] = jnp.zeros_like(dr)
    for copy in loads:
        copy.wait()
    arrive(near)
    arrive([cross4])
    arrive(third)

    for n in range(2):
        for j in range(SEL):
            owner, part = lax.div(ids[n, j], 3), lax.rem(ids[n, j], 3)
            for r in range(4):
                k[n, 64 * j + 16 * r : 64 * j + 16 * r + 16, :LAT] = kc[owner, 4 * part + r]
            for r in range(2):
                packs = kc[owner, 12 + r].astype(F32)
                pack = packs[:, 256:384]
                pack = jnp.where(part == 0, packs[:, 0:128], pack)
                pack = jnp.where(part == 1, packs[:, 128:256], pack)
                low, high = pack[:, :64].astype(BF), pack[:, 64:].astype(BF)
                row = 64 * j + 16 * r
                k[n, row : row + 16, LAT:] = jnp.concatenate([low, low], axis=1)
                k[n, row + 32 : row + 48, LAT:] = jnp.concatenate([high, high], axis=1)
        kt[n] = k[n, :, :LAT].T

    first_swap = links.count
    links.count += 8

    def swap(i):
        return pltpu.make_async_remote_copy(
            src_ref=d.at[:, 1 - core, :, :, i],
            dst_ref=core_in.at[:, :, :, i],
            send_sem=send.at[first_swap + i],
            recv_sem=recv.at[first_swap + i],
            device_id=links.to["core"][0],
            device_id_type=MESH,
        )

    def add(dst, *srcs):
        total = dst[...].astype(F32)
        for src in srcs:
            total = total + src[...].astype(F32)
        dst[...] = total.astype(BF)

    def swap_add(i):
        swap(i).wait_recv()
        for part in (0, 1):
            for n in range(4):
                add(d.at[part, core, n, :, i], core_in.at[part, n, :, i])

    def p_send1(h, start=True):
        out = []
        for part, way in ((0, "y"), (1, "x")):
            for side in (0, 1):
                ref = d.at[part, core, (mine[part] + 2) % 4, pl.ds(2 * side, 2), pl.ds(4 * h, 4)]
                out.append(links.push(ref, p1.at[h, part, side], way, side, start))
        return out

    def p_add1(h):
        for part in (0, 1):
            for side, sign in ((0, 1), (1, -1)):
                o = (mine[part] + sign + 4) % 4
                for n in range(2):
                    add(d.at[part, core, o, 2 * side + n, pl.ds(4 * h, 4)], p1.at[h, part, side, n])

    def p_send2(h, start=True):
        out = []
        for part, way in ((0, "y"), (1, "x")):
            for side, sign in ((0, 1), (1, -1)):
                ref = d.at[part, core, (mine[part] + sign + 4) % 4, :, pl.ds(4 * h, 4)]
                out.append(links.push(ref, p2.at[h, part, side], way, side, start))
        return out

    def p_add2(h):
        for part in (0, 1):
            for n in range(4):
                ref = d.at[part, core, mine[part], n, pl.ds(4 * h, 4)]
                add(ref, p2.at[h, part, 0, n], p2.at[h, part, 1, n])

    def q_send1():
        out = []
        for part, way in ((0, "x"), (1, "y")):
            o = (mine[1 - part] + 2) % 4
            for side in (0, 1):
                rows = pl.ds(4 * side, 4)
                out.append(links.push(d.at[part, core, mine[part], o, rows], q1.at[part, side], way, side))
        return out

    def q_add1():
        for part in (0, 1):
            for side, sign in ((0, 1), (1, -1)):
                o = (mine[1 - part] + sign + 4) % 4
                add(d.at[part, core, mine[part], o, pl.ds(4 * side, 4)], q1.at[part, side])

    def q_send2():
        out = []
        for part, way in ((0, "x"), (1, "y")):
            for side, sign in ((0, 1), (1, -1)):
                o = (mine[1 - part] + sign + 4) % 4
                out.append(links.push(d.at[part, core, mine[part], o], q2.at[part, side], way, side))
        return out

    def q_add2():
        for part in (0, 1):
            add(d.at[part, core, mine[part], mine[1 - part]], q2.at[part, 0], q2.at[part, 1])

    def total_of(part):
        total = d[part, core, mine[part], mine[1 - part], z].astype(F32)
        for n in range(7):
            total = total + zin[part, n].astype(F32)
        return total

    yc2 = ring_y2(2, False)
    late = [share(1, False), share(3, False), share(2, False)]
    pa1 = p_send1(0, False)

    @pl.loop(0, 8)
    def _(i):
        forward(i, q, qr, og, k, kt, bias, ph, d)
        swap(i).start()

        @pl.when(i > 0)
        def _():
            swap_add(i - 1)

        @pl.when(i == 0)
        def _():
            arrive(yc)
            for copy in yc2:
                copy.start()
            late[0].start()
            late[1].start()

        @pl.when(i == 4)
        def _():
            for copy in pa1:
                copy.start()

        @pl.when(i == 5)
        def _():
            arrive(ya2)
            arrive(yb2)
            arrive(yc2)
            late[2].start()

    swap_add(7)
    pb1 = p_send1(1)
    arrive(shared)
    pa2, pb2 = p_send2(0, False), p_send2(1, False)

    @pl.loop(0, 8)
    def _(i):
        backward(i, q, qr, og, k, g, ph, dk, dr)

        @pl.when(i == 0)
        def _():
            arrive(pa1)
            p_add1(0)
            for copy in pa2:
                copy.start()

        @pl.when(i == 2)
        def _():
            arrive(pb1)
            p_add1(1)
            for copy in pb2:
                copy.start()

        @pl.when(i == 6)
        def _():
            arrive(pa2)
            p_add2(0)

    links.finish()
    links.started = []
    for n in range(2):
        for j in range(SEL):
            fold = dr[n, 64 * j : 64 * j + 64, :]
            fold = fold[:, :64] + fold[:, 64:]
            drp[SEL * n + j] = jnp.concatenate([fold[:32], fold[32:]], axis=1)

    def fill(o):
        hits = [
            [jnp.where(ids[n, j] == o * 3 + part, 1.0, 0.0).astype(F32) for n in range(2) for j in range(SEL)]
            for part in range(3)
        ]
        packs = []
        for part in range(3):
            pack = jnp.zeros((32, 128), F32)
            for n in range(2 * SEL):
                pack = pack + hits[part][n] * drp[n]
            packs.append(pack.astype(BF))
            for r in range(4):
                total = jnp.zeros((16, LAT), F32)
                for n in range(2 * SEL):
                    low = 64 * (n % SEL) + 16 * r
                    total = total + hits[part][n] * dk[n // SEL, low : low + 16, :]
                kc[o, 4 * part + r] = total.astype(BF)
        packs = jnp.concatenate(packs + [jnp.zeros((32, 128), BF)], axis=1)
        kc[o, 12] = packs[:16]
        kc[o, 13] = packs[16:]

    def away(o, slot, way, side=0, rows=None):
        src, dst = kc.at[o], cin.at[slot]
        if rows is not None:
            src, dst = src.at[rows], dst.at[rows]
        return links.push(src, dst, way, side)

    def take(o, slots, rows=slice(None)):
        total = kc[o, rows].astype(F32)
        for slot in slots:
            total = total + cin[slot, rows].astype(F32)
        kc[o, rows] = total.astype(BF)

    lower, higher = slice(0, HALF), slice(HALF, TILES)
    fill(oth(4))
    cross4 = away(oth(4), 0, "far")
    fill(oth(3))
    fill(oth(-3))
    third = [away(oth(3), 1, "z", 0), away(oth(-3), 2, "z", 1)]
    fill(oth(2))
    fill(oth(-2))
    fill(own(4))
    arrive(pb2)
    p_add2(1)
    w = q_send1()
    arrive(third)
    take(oth(2), [1])
    take(oth(-2), [2])
    cross2 = [away(oth(2), 3, "far"), away(oth(-2), 4, "far")]
    arrive([cross4])
    take(own(4), [0])
    c = [away(own(4), 5, "z", 0, upper(0)), away(own(4), 6, "z", 1, upper(1))]
    fill(own(3))
    fill(own(-3))
    arrive(c)
    take(own(3), [5], lower)
    take(own(-3), [6], higher)
    c = [away(own(3), 7, "z", 0), away(own(-3), 8, "z", 1)]
    arrive(w)
    q_add1()
    w = q_send2()
    fill(oth(1))
    fill(oth(-1))
    near = [away(oth(1), 9, "z", 0, upper(1)), away(oth(-1), 10, "z", 1, upper(0))]
    cross1 = [away(oth(1), 11, "far", 0, upper(0)), away(oth(-1), 12, "far", 0, upper(1))]
    fill(own(2))
    fill(own(-2))
    fill(oth(0))
    arrive(c)
    arrive(cross2)
    take(own(2), [7, 3])
    take(own(-2), [8, 4])
    c = [away(own(2), 13, "z", 0), away(own(-2), 14, "z", 1)]
    arrive(near)
    take(oth(0), [9], higher)
    take(oth(0), [10], lower)
    cross0 = away(oth(0), 15, "far")
    arrive(w)
    q_add2()
    w = [
        links.push(
            d.at[part, core, mine[part], mine[1 - part], (z + n) % 8], zin.at[part, n - 1], ("z", n)
        )
        for n in (4, 3, 5, 2, 6, 1, 7)
        for part in (0, 1)
    ]
    fill(own(1))
    fill(own(-1))
    fill(own(0))
    arrive(cross1)
    take(own(1), [11], lower)
    take(own(-1), [12], higher)
    arrive(c)
    take(own(1), [13])
    take(own(-1), [14])
    c = [away(own(1), 16, "z", 0), away(own(-1), 17, "z", 1)]
    arrive(w)
    wg[0:64, :] = total_of(0)
    wg[64:128, :] = total_of(1)
    arrive([cross0])
    arrive(c)
    total = kc[own(0)].astype(F32)
    for slot in (15, 16, 17):
        total = total + cin[slot].astype(F32)
    cg[...] = total[0:12].astype(BF)
    pack = total[12:14].reshape(32, LAT)
    rows = [pack[:, 64 * i : 64 * i + 64] for i in range(6)] + [jnp.zeros((64, ROPE), F32)]
    flipped = jnp.concatenate(rows, axis=0)
    flipped = jnp.concatenate([flipped, jnp.zeros((256, 128 - ROPE), F32)], axis=1).T
    rg[...] = flipped[:ROPE, :192].astype(BF)
    links.finish()

    @pl.loop(0, 8)
    def _(i):
        swap(i).wait_send()


def finish_kernel(cg, rg, wg, cg_out, rg_out, wg_out, sem):
    pairs = ((cg, cg_out), (rg, rg_out), (wg, wg_out))
    copies = [pltpu.make_async_copy(src, dst, sem.at[n]) for n, (src, dst) in enumerate(pairs)]
    for copy in copies:
        copy.start()
    for copy in copies:
        copy.wait()


def finish(*arrays):
    return pl.pallas_call(
        finish_kernel,
        out_shape=tuple(jax.ShapeDtypeStruct(a.shape, a.dtype) for a in arrays),
        in_specs=[pl.BlockSpec(memory_space=pl.ANY)] * 3,
        out_specs=(pl.BlockSpec(memory_space=pl.ANY),) * 3,
        scratch_shapes=[pltpu.SemaphoreType.DMA((3,))],
        compiler_params=pltpu.CompilerParams(vmem_limit_bytes=63 * 2**20),
        name="finish",
    )(*arrays)


def run(ids, counts, cache, rope, weight, q, qr, og):
    return pl.pallas_call(
        core_kernel,
        out_shape=(
            jax.ShapeDtypeStruct((12, 16, LAT), BF),
            jax.ShapeDtypeStruct((ROPE, 192), BF),
            jax.ShapeDtypeStruct((128, HD), F32),
        ),
        in_specs=[pl.BlockSpec(memory_space=pltpu.SMEM)] * 2 + [pl.BlockSpec(memory_space=pl.ANY)] * 6,
        out_specs=(pl.BlockSpec(memory_space=pltpu.VMEM),) * 3,
        scratch_shapes=[
            pltpu.VMEM((16, TILES, 16, LAT), BF),
            pltpu.VMEM((2, 4, 4, 8, 128, HD), BF),
            pltpu.VMEM((2, 2, 4, 4, 8, 64, HD), BF),
            pltpu.VMEM((2, 4, 4, 8, 64, HD), BF),
            pltpu.VMEM((128, 64 * LAT), BF),
            pltpu.VMEM((128, 64 * ROPE), BF),
            pltpu.VMEM((128, 64 * HD), BF),
            pltpu.VMEM((ROPE, 192), BF),
            pltpu.VMEM((2, 256, LAT + 128), BF),
            pltpu.VMEM((2, LAT, 256), BF),
            pltpu.VMEM((2, 256, 128), F32),
            pltpu.VMEM((8, 2, 256, 512), BF),
            pltpu.VMEM((2, 256, LAT), F32),
            pltpu.VMEM((2, 256, 128), F32),
            pltpu.VMEM((2 * SEL, 32, 128), F32),
            pltpu.VMEM((18, TILES, 16, LAT), BF),
            pltpu.VMEM((2, 2, 2, 2, 4, 64, HD), BF),
            pltpu.VMEM((2, 2, 2, 4, 4, 64, HD), BF),
            pltpu.VMEM((2, 2, 4, 64, HD), BF),
            pltpu.VMEM((2, 2, 8, 64, HD), BF),
            pltpu.VMEM((2, 7, 64, HD), BF),
            pltpu.SemaphoreType.DMA((130,)),
            pltpu.SemaphoreType.DMA((130,)),
            pltpu.SemaphoreType.DMA((7,)),
        ],
        compiler_params=pltpu.CompilerParams(
            collective_id=0, has_side_effects=True, vmem_limit_bytes=63 * 2**20
        ),
        name="whole",
    )(ids, counts, cache, rope, weight, q, qr, og)


def shards(
    q_latent,
    q_rope,
    latent_cache,
    rope_keys,
    up_weight,
    out_grad,
    block_ids,
    block_counts,
    slab_offset,
):
    cg, rg, wg = finish(*run(
        block_ids[0],
        block_counts[0],
        latent_cache.reshape(12, 16, LAT),
        rope_keys[0].T,
        up_weight.reshape(128, HD),
        q_latent[0],
        q_rope[0],
        out_grad[0],
    ))
    return cg.reshape(1, 192, LAT), rg.T[None], wg.reshape(4, 32, HD)


def solution(mesh):
    placed = (
        P("dp", "ctx", None),
        P("dp", "ctx", None),
        P("dp", "ctx", None),
        P("dp", "ctx", None),
        P("ctx", "dp", None),
        P("dp", "ctx", None),
        P("dp", "ctx", None),
        P("dp", "ctx"),
        P("dp"),
    )
    return jax.shard_map(
        shards,
        mesh=mesh,
        in_specs=placed,
        out_specs=(P("dp", "ctx", None), P("dp", "ctx", None), P("ctx", "dp", None)),
        check_vma=False,
    )
```

```python
import functools

import jax
import jax.numpy as jnp
from jax import lax
from jax.experimental import pallas as pl
from jax.experimental.pallas import tpu as pltpu
from jax.sharding import PartitionSpec as P

LAT = 512
ROPE = 64
HD = 128
BLK = 64
SEL = 4
SCALE = (HD + ROPE) ** (-0.5)
TILES = 14
HALF = TILES // 2
MESH = pl.DeviceIdType.MESH
BF = jnp.bfloat16
F32 = jnp.float32


def place():
    dp, ctx = lax.axis_index("dp"), lax.axis_index("ctx")
    core, y, x_lo = dp % 2, (dp // 2) % 4, dp // 8
    x_hi, z = ctx // 8, ctx % 8
    return x_hi * 2 + x_lo, y, z, core, x_hi


def device(x, y, z, core):
    return (((x % 2) * 4 + y) * 2 + core, (x // 2) * 8 + z)


class Links:
    def __init__(self, send, recv):
        x, y, z, core, _ = place()
        self.send, self.recv, self.count, self.started = send, recv, 0, []
        self.to = {
            "z": (device(x, y, (z + 1) % 8, core), device(x, y, (z + 7) % 8, core)),
            "y": (device(x, (y + 1) % 4, z, core), device(x, (y + 3) % 4, z, core)),
            "x": (device((x + 1) % 4, y, z, core), device((x + 3) % 4, y, z, core)),
            "far": (device((x + 2) % 4, y, z, core),),
            "core": (device(x, y, z, 1 - core),),
        }
        for n in range(1, 8):
            self.to["z", n] = (device(x, y, (z + n) % 8, core),)

    def barrier(self):
        sem = pltpu.get_barrier_semaphore()
        partners = [d for way, group in self.to.items() if way != "z" for d in group]
        for d in partners:
            pl.semaphore_signal(sem, inc=1, device_id=d, device_id_type=MESH)
        pl.semaphore_wait(sem, len(partners))

    def push(self, src, dst, way, side=0, start=True):
        i = self.count
        self.count += 1
        copy = pltpu.make_async_remote_copy(
            src_ref=src,
            dst_ref=dst,
            send_sem=self.send.at[i],
            recv_sem=self.recv.at[i],
            device_id=self.to[way][side],
            device_id_type=MESH,
        )
        if start:
            copy.start()
        self.started.append(copy)
        return copy

    def finish(self):
        for copy in self.started:
            copy.wait_send()


def arrive(copies):
    for copy in copies:
        copy.wait_recv()


NT = (((1,), (1,)), ((), ()))
NN = (((1,), (0,)), ((), ()))


def dot(a, b, dims):
    return lax.dot_general(a, b, dims, preferred_element_type=F32)


def lanes_of(c, width):
    return pl.ds(pl.multiple_of(c * width, width), width)


SPOTS = [(x_lo, y, core) for x_lo in range(2) for y in range(4) for core in range(2)]


def weight_at(part, xh, x_lo, y, core, z):
    return (core, y, 2 * xh + x_lo, z, slice(64 * part, 64 * part + 64))


def grad_at(part, xh, x_lo, y, core, z):
    xx = 2 * xh + x_lo
    return (0, core, y, xx, z) if part == 0 else (1, core, xx, y, z)


def grads_of_pair(og, i, xh, part):
    low = og[:, lanes_of((xh * 8 + i) * 2 + part, 2 * HD)]
    zero = jnp.zeros((64, HD), BF)
    rows = []
    for b in range(2):
        first, second = low[64 * b : 64 * b + 64, :HD], low[64 * b : 64 * b + 64, HD:]
        rows.append(jnp.concatenate([first, zero], axis=1))
        rows.append(jnp.concatenate([zero, second], axis=1))
    return jnp.concatenate(rows, axis=0)


def queries(q, i, b):
    parts = []
    for xh in range(2):
        block = q[64 * b : 64 * b + 64, lanes_of(xh * 8 + i, 4 * LAT)]
        parts += [block[:, LAT * j : LAT * j + LAT] for j in range(4)]
    return jnp.concatenate(parts, axis=0)


def rotary(qr, i, b):
    low = lax.broadcasted_iota(jnp.int32, (64, 128), 1) < 64
    parts = []
    for xh in range(2):
        block = qr[64 * b : 64 * b + 64, lanes_of(xh * 8 + i, 4 * ROPE)].astype(F32)
        for j in range(4):
            slab = block[:, 128 * (j // 2) : 128 * (j // 2) + 128]
            slab = jnp.where(low, slab, 0.0) if j % 2 == 0 else jnp.where(low, 0.0, slab)
            parts.append(slab.astype(BF))
    return jnp.concatenate(parts, axis=0)


def scores(i, q, qr, k, bias, ph):
    for b in range(2):
        qs = jnp.concatenate([queries(q, i, b), rotary(qr, i, b)], axis=1)
        s = dot(k[b], qs, NT) * SCALE + jnp.concatenate([bias[b]] * 4, axis=1)
        e = jnp.exp(s - jnp.max(s, axis=0, keepdims=True))
        ph[i, b] = (e * (1.0 / jnp.sum(e, axis=0, keepdims=True))).astype(BF)


def outputs(i, og, kt, ph, d):
    outs = [dot(kt[b], ph[i, b], NN).astype(BF) for b in range(2)]
    for pair in range(4):
        xh, part = pair // 2, pair % 2
        both = jnp.concatenate([out[:, 128 * pair : 128 * pair + 128] for out in outs], axis=1)
        dw = dot(both, grads_of_pair(og, i, xh, part), NN).astype(BF)
        for n, spot in enumerate(SPOTS):
            rows = dw[32 * n : 32 * n + 32]
            d[grad_at(part, xh, *spot, i)] = jnp.concatenate([rows[:, :HD], rows[:, HD:]], axis=0)


def backward(i, q, qr, og, k, w, ph, dk, dr):
    backs = []
    for pair in range(4):
        xh, part = pair // 2, pair % 2
        pieces = [w[weight_at(part, xh, *spot, i)] for spot in SPOTS]
        weight = jnp.concatenate(
            [jnp.concatenate([p[:32], p[32:]], axis=1) for p in pieces], axis=0
        )
        backs.append(dot(grads_of_pair(og, i, xh, part), weight, NT).astype(BF))
    for b in range(2):
        back = jnp.concatenate([back[128 * b : 128 * b + 128] for back in backs], axis=0)
        dp = dot(k[b, :, :LAT], back, NT)
        half = ph[i, b]
        prob = half.astype(F32)
        weighted = prob * dp
        delta = jnp.sum(weighted, axis=0, keepdims=True)
        ds = ((weighted - prob * delta) * SCALE).astype(BF)
        dk[b] += dot(
            jnp.concatenate([half, ds], axis=1), jnp.concatenate([back, queries(q, i, b)], axis=0), NN
        )
        dr[b] += dot(ds, rotary(qr, i, b), NN)


def core_kernel(
    ids, counts, cache, rope, w_in, q_hbm, qr_hbm, og_hbm, cg, rg, wg,
    kc, g, d, core_in, q, qr, og, rope_v, k, kt, bias, ph, dk, dr, drp, cin, p1, p2, q1, q2, zin,
    send, recv, lsem,
):
    x, y, z, core, xh = place()
    links = Links(send, recv)
    mine = (y, x)

    def own(n):
        return xh * 8 + (z + n + 8) % 8

    def oth(n):
        return (1 - xh) * 8 + (z + n + 8) % 8

    def upper(side):
        return pl.ds(HALF * side, HALF)

    first = [
        pltpu.make_async_copy(cache, kc.at[own(0), pl.ds(0, 12)], lsem.at[0]),
        pltpu.make_async_copy(rope, rope_v, lsem.at[1]),
        pltpu.make_async_copy(w_in, g.at[core, y, x, z], lsem.at[2]),
    ]
    loads = [
        pltpu.make_async_copy(qr_hbm, qr, lsem.at[4]),
        pltpu.make_async_copy(og_hbm, og, lsem.at[5]),
        pltpu.make_async_copy(q_hbm, q, lsem.at[6]),
    ]
    for copy in first + loads:
        copy.start()
    links.barrier()
    for copy in first:
        copy.wait()
    flipped = jnp.concatenate([rope_v[...].astype(F32), jnp.zeros((ROPE, 64), F32)], axis=1)
    flipped = jnp.concatenate([flipped, jnp.zeros((128 - ROPE, 256), F32)], axis=0).T
    packed = [flipped[32 * i : 32 * i + 32, :ROPE].astype(BF) for i in range(6)]
    packed = jnp.concatenate(packed + [jnp.zeros((32, 128), BF)], axis=1)
    kc[own(0), 12] = packed[:16]
    kc[own(0), 13] = packed[16:]

    def ring_x(s):
        out = []
        for side, sign in ((0, 1), (1, -1)):
            if s == 1:
                ref = g.at[core, y, x]
            else:
                ref = g.at[core, y, (x - sign + 4) % 4, pl.ds(4 * side, 4)]
            out.append(links.push(ref, ref, "x", side))
        return out

    def ring_y1(n):
        ref = g.at[core, y, (x + n + 4) % 4]
        return [links.push(ref, ref, "y", side) for side in (0, 1)]

    def ring_y2(n, start=True):
        out = []
        for side, sign in ((0, 1), (1, -1)):
            ref = g.at[core, (y - sign + 4) % 4, (x + n + 4) % 4, pl.ds(4 * side, 4)]
            out.append(links.push(ref, ref, "y", side, start))
        return out

    shared = []

    def share(n, start=True):
        ref = g.at[core, (y + n) % 4]
        shared.append(links.push(ref, ref, "core", 0, start))
        return shared[-1]

    def ring8(s):
        out = []
        for side, sign in ((0, 1), (1, -1)):
            ref = kc.at[own(-sign * (s - 1))]
            if s == 4:
                ref = ref.at[upper(side)]
            out.append(links.push(ref, ref, "z", side))
        return out

    def push_block(o, way, side=0, rows=None):
        ref = kc.at[o]
        if rows is not None:
            ref = ref.at[rows]
        return links.push(ref, ref, way, side)

    weights = g.at[core, y, x, z]
    c = ring8(1)
    cross0 = push_block(own(0), "far")
    wz = [links.push(weights, weights, ("z", n)) for n in (4, 3, 5, 2, 6, 1, 7)]
    arrive(c)
    c = ring8(2)
    arrive(wz)
    ya = ring_y1(0)
    wx = ring_x(1)
    arrive([cross0])
    near = [push_block(oth(0), "z", 0), push_block(oth(0), "z", 1)]
    arrive(c)
    c = ring8(3)
    cross2 = [push_block(own(2), "far"), push_block(own(-2), "far")]
    arrive(ya)
    ya2 = ring_y2(0)
    arrive(wx)
    wx = ring_x(2)
    yb = ring_y1(1) + ring_y1(-1)
    arrive(c)
    c = ring8(4)
    arrive(c)
    cross4 = push_block(own(4), "far")
    arrive(wx)
    yc = ring_y1(2)
    share(0)
    arrive(cross2)
    third = [push_block(oth(-2), "z", 0), push_block(oth(2), "z", 1)]
    arrive(yb)
    yb2 = ring_y2(1) + ring_y2(-1)
    row = lax.broadcasted_iota(jnp.int32, (256, 128), 0)
    col = lax.broadcasted_iota(jnp.int32, (256, 128), 1)
    for n in range(2):
        slot = row // 64
        causal = jnp.where(row % 64 <= col % 64, 0.0, -1e30).astype(F32)
        listed = jnp.where(slot < counts[n], 0.0, -1e30).astype(F32)
        bias[n] = jnp.where(slot == 0, causal, listed)
    dk[...] = jnp.zeros_like(dk)
    dr[...] = jnp.zeros_like(dr)
    for copy in loads:
        copy.wait()
    arrive(near)
    arrive([cross4])
    arrive(third)

    for n in range(2):
        for j in range(SEL):
            owner, part = lax.div(ids[n, j], 3), lax.rem(ids[n, j], 3)
            for r in range(4):
                k[n, 64 * j + 16 * r : 64 * j + 16 * r + 16, :LAT] = kc[owner, 4 * part + r]
            for r in range(2):
                packs = kc[owner, 12 + r].astype(F32)
                pack = packs[:, 256:384]
                pack = jnp.where(part == 0, packs[:, 0:128], pack)
                pack = jnp.where(part == 1, packs[:, 128:256], pack)
                low, high = pack[:, :64].astype(BF), pack[:, 64:].astype(BF)
                row = 64 * j + 16 * r
                k[n, row : row + 16, LAT:] = jnp.concatenate([low, low], axis=1)
                k[n, row + 32 : row + 48, LAT:] = jnp.concatenate([high, high], axis=1)
        kt[n] = k[n, :, :LAT].T

    first_swap = links.count
    links.count += 8

    def swap(i):
        return pltpu.make_async_remote_copy(
            src_ref=d.at[:, 1 - core, :, :, i],
            dst_ref=core_in.at[:, :, :, i],
            send_sem=send.at[first_swap + i],
            recv_sem=recv.at[first_swap + i],
            device_id=links.to["core"][0],
            device_id_type=MESH,
        )

    def add(dst, *srcs):
        total = dst[...].astype(F32)
        for src in srcs:
            total = total + src[...].astype(F32)
        dst[...] = total.astype(BF)

    def swap_add(i):
        swap(i).wait_recv()
        for part in (0, 1):
            for n in range(4):
                add(d.at[part, core, n, :, i], core_in.at[part, n, :, i])

    def p_send1(h, start=True):
        out = []
        for part, way in ((0, "y"), (1, "x")):
            for side in (0, 1):
                ref = d.at[part, core, (mine[part] + 2) % 4, pl.ds(2 * side, 2), pl.ds(4 * h, 4)]
                out.append(links.push(ref, p1.at[h, part, side], way, side, start))
        return out

    def p_add1(h):
        for part in (0, 1):
            for side, sign in ((0, 1), (1, -1)):
                o = (mine[part] + sign + 4) % 4
                for n in range(2):
                    add(d.at[part, core, o, 2 * side + n, pl.ds(4 * h, 4)], p1.at[h, part, side, n])

    def p_send2(h, start=True):
        out = []
        for part, way in ((0, "y"), (1, "x")):
            for side, sign in ((0, 1), (1, -1)):
                ref = d.at[part, core, (mine[part] + sign + 4) % 4, :, pl.ds(4 * h, 4)]
                out.append(links.push(ref, p2.at[h, part, side], way, side, start))
        return out

    def p_add2(h):
        for part in (0, 1):
            for n in range(4):
                ref = d.at[part, core, mine[part], n, pl.ds(4 * h, 4)]
                add(ref, p2.at[h, part, 0, n], p2.at[h, part, 1, n])

    def q_send1():
        out = []
        for part, way in ((0, "x"), (1, "y")):
            o = (mine[1 - part] + 2) % 4
            for side in (0, 1):
                rows = pl.ds(4 * side, 4)
                out.append(links.push(d.at[part, core, mine[part], o, rows], q1.at[part, side], way, side))
        return out

    def q_add1():
        for part in (0, 1):
            for side, sign in ((0, 1), (1, -1)):
                o = (mine[1 - part] + sign + 4) % 4
                add(d.at[part, core, mine[part], o, pl.ds(4 * side, 4)], q1.at[part, side])

    def q_send2():
        out = []
        for part, way in ((0, "x"), (1, "y")):
            for side, sign in ((0, 1), (1, -1)):
                o = (mine[1 - part] + sign + 4) % 4
                out.append(links.push(d.at[part, core, mine[part], o], q2.at[part, side], way, side))
        return out

    def q_add2():
        for part in (0, 1):
            add(d.at[part, core, mine[part], mine[1 - part]], q2.at[part, 0], q2.at[part, 1])

    def total_of(part):
        total = d[part, core, mine[part], mine[1 - part], z].astype(F32)
        for n in range(7):
            total = total + zin[part, n].astype(F32)
        return total

    yc2 = ring_y2(2, False)
    late = [share(1, False), share(3, False), share(2, False)]
    pa1 = p_send1(0, False)

    scores(0, q, qr, k, bias, ph)

    @pl.loop(1, 8)
    def _(i):
        scores(i, q, qr, k, bias, ph)
        outputs(i - 1, og, kt, ph, d)
        swap(i - 1).start()

        @pl.when(i > 1)
        def _():
            swap_add(i - 2)

        @pl.when(i == 1)
        def _():
            arrive(yc)
            for copy in yc2:
                copy.start()
            late[0].start()
            late[1].start()

        @pl.when(i == 5)
        def _():
            for copy in pa1:
                copy.start()

        @pl.when(i == 6)
        def _():
            arrive(ya2)
            arrive(yb2)
            arrive(yc2)
            late[2].start()

    outputs(7, og, kt, ph, d)
    swap(7).start()
    swap_add(6)
    swap_add(7)
    pb1 = p_send1(1)
    arrive(shared)
    pa2, pb2 = p_send2(0, False), p_send2(1, False)

    @pl.loop(0, 8)
    def _(i):
        backward(i, q, qr, og, k, g, ph, dk, dr)

        @pl.when(i == 0)
        def _():
            arrive(pa1)
            p_add1(0)
            for copy in pa2:
                copy.start()

        @pl.when(i == 2)
        def _():
            arrive(pb1)
            p_add1(1)
            for copy in pb2:
                copy.start()

        @pl.when(i == 6)
        def _():
            arrive(pa2)
            p_add2(0)

    links.finish()
    links.started = []
    for n in range(2):
        for j in range(SEL):
            fold = dr[n, 64 * j : 64 * j + 64, :]
            fold = fold[:, :64] + fold[:, 64:]
            drp[SEL * n + j] = jnp.concatenate([fold[:32], fold[32:]], axis=1)

    def fill(o):
        hits = [
            [jnp.where(ids[n, j] == o * 3 + part, 1.0, 0.0).astype(F32) for n in range(2) for j in range(SEL)]
            for part in range(3)
        ]
        packs = []
        for part in range(3):
            pack = jnp.zeros((32, 128), F32)
            for n in range(2 * SEL):
                pack = pack + hits[part][n] * drp[n]
            packs.append(pack.astype(BF))
            for r in range(4):
                total = jnp.zeros((16, LAT), F32)
                for n in range(2 * SEL):
                    low = 64 * (n % SEL) + 16 * r
                    total = total + hits[part][n] * dk[n // SEL, low : low + 16, :]
                kc[o, 4 * part + r] = total.astype(BF)
        packs = jnp.concatenate(packs + [jnp.zeros((32, 128), BF)], axis=1)
        kc[o, 12] = packs[:16]
        kc[o, 13] = packs[16:]

    def away(o, slot, way, side=0, rows=None):
        src, dst = kc.at[o], cin.at[slot]
        if rows is not None:
            src, dst = src.at[rows], dst.at[rows]
        return links.push(src, dst, way, side)

    def take(o, slots, rows=slice(None)):
        total = kc[o, rows].astype(F32)
        for slot in slots:
            total = total + cin[slot, rows].astype(F32)
        kc[o, rows] = total.astype(BF)

    lower, higher = slice(0, HALF), slice(HALF, TILES)
    fill(oth(4))
    cross4 = away(oth(4), 0, "far")
    fill(oth(3))
    fill(oth(-3))
    third = [away(oth(3), 1, "z", 0), away(oth(-3), 2, "z", 1)]
    fill(oth(2))
    fill(oth(-2))
    fill(own(4))
    arrive(pb2)
    p_add2(1)
    w = q_send1()
    arrive(third)
    take(oth(2), [1])
    take(oth(-2), [2])
    cross2 = [away(oth(2), 3, "far"), away(oth(-2), 4, "far")]
    arrive([cross4])
    take(own(4), [0])
    c = [away(own(4), 5, "z", 0, upper(0)), away(own(4), 6, "z", 1, upper(1))]
    fill(own(3))
    fill(own(-3))
    arrive(c)
    take(own(3), [5], lower)
    take(own(-3), [6], higher)
    c = [away(own(3), 7, "z", 0), away(own(-3), 8, "z", 1)]
    arrive(w)
    q_add1()
    w = q_send2()
    fill(oth(1))
    fill(oth(-1))
    near = [away(oth(1), 9, "z", 0, upper(1)), away(oth(-1), 10, "z", 1, upper(0))]
    cross1 = [away(oth(1), 11, "far", 0, upper(0)), away(oth(-1), 12, "far", 0, upper(1))]
    fill(own(2))
    fill(own(-2))
    fill(oth(0))
    arrive(c)
    arrive(cross2)
    take(own(2), [7, 3])
    take(own(-2), [8, 4])
    c = [away(own(2), 13, "z", 0), away(own(-2), 14, "z", 1)]
    arrive(near)
    take(oth(0), [9], higher)
    take(oth(0), [10], lower)
    cross0 = away(oth(0), 15, "far")
    arrive(w)
    q_add2()
    w = [
        links.push(
            d.at[part, core, mine[part], mine[1 - part], (z + n) % 8], zin.at[part, n - 1], ("z", n)
        )
        for n in (4, 3, 5, 2, 6, 1, 7)
        for part in (0, 1)
    ]
    fill(own(1))
    fill(own(-1))
    fill(own(0))
    arrive(cross1)
    take(own(1), [11], lower)
    take(own(-1), [12], higher)
    arrive(c)
    take(own(1), [13])
    take(own(-1), [14])
    c = [away(own(1), 16, "z", 0), away(own(-1), 17, "z", 1)]
    arrive(w)
    wg[0:64, :] = total_of(0)
    wg[64:128, :] = total_of(1)
    arrive([cross0])
    arrive(c)
    total = kc[own(0)].astype(F32)
    for slot in (15, 16, 17):
        total = total + cin[slot].astype(F32)
    cg[...] = total[0:12].astype(BF)
    pack = total[12:14].reshape(32, LAT)
    rows = [pack[:, 64 * i : 64 * i + 64] for i in range(6)] + [jnp.zeros((64, ROPE), F32)]
    flipped = jnp.concatenate(rows, axis=0)
    flipped = jnp.concatenate([flipped, jnp.zeros((256, 128 - ROPE), F32)], axis=1).T
    rg[...] = flipped[:ROPE, :192].astype(BF)
    links.finish()

    @pl.loop(0, 8)
    def _(i):
        swap(i).wait_send()


def finish_kernel(cg, rg, wg, cg_out, rg_out, wg_out):
    cg_out[...] = cg[...]
    rg_out[...] = rg[...]
    wg_out[...] = wg[...]


def finish(*arrays):
    return pl.pallas_call(
        finish_kernel,
        out_shape=tuple(jax.ShapeDtypeStruct(a.shape, a.dtype) for a in arrays),
        in_specs=[pl.BlockSpec(memory_space=pltpu.VMEM)] * 3,
        out_specs=(pl.BlockSpec(memory_space=pltpu.VMEM),) * 3,
        name="finish",
    )(*arrays)


def run(ids, counts, cache, rope, weight, q, qr, og):
    return pl.pallas_call(
        core_kernel,
        out_shape=(
            jax.ShapeDtypeStruct((12, 16, LAT), BF),
            jax.ShapeDtypeStruct((ROPE, 192), BF),
            jax.ShapeDtypeStruct((128, HD), F32),
        ),
        in_specs=[pl.BlockSpec(memory_space=pltpu.SMEM)] * 2 + [pl.BlockSpec(memory_space=pl.ANY)] * 6,
        out_specs=(pl.BlockSpec(memory_space=pltpu.VMEM),) * 3,
        scratch_shapes=[
            pltpu.VMEM((16, TILES, 16, LAT), BF),
            pltpu.VMEM((2, 4, 4, 8, 128, HD), BF),
            pltpu.VMEM((2, 2, 4, 4, 8, 64, HD), BF),
            pltpu.VMEM((2, 4, 4, 8, 64, HD), BF),
            pltpu.VMEM((128, 64 * LAT), BF),
            pltpu.VMEM((128, 64 * ROPE), BF),
            pltpu.VMEM((128, 64 * HD), BF),
            pltpu.VMEM((ROPE, 192), BF),
            pltpu.VMEM((2, 256, LAT + 128), BF),
            pltpu.VMEM((2, LAT, 256), BF),
            pltpu.VMEM((2, 256, 128), F32),
            pltpu.VMEM((8, 2, 256, 512), BF),
            pltpu.VMEM((2, 256, LAT), F32),
            pltpu.VMEM((2, 256, 128), F32),
            pltpu.VMEM((2 * SEL, 32, 128), F32),
            pltpu.VMEM((18, TILES, 16, LAT), BF),
            pltpu.VMEM((2, 2, 2, 2, 4, 64, HD), BF),
            pltpu.VMEM((2, 2, 2, 4, 4, 64, HD), BF),
            pltpu.VMEM((2, 2, 4, 64, HD), BF),
            pltpu.VMEM((2, 2, 8, 64, HD), BF),
            pltpu.VMEM((2, 7, 64, HD), BF),
            pltpu.SemaphoreType.DMA((130,)),
            pltpu.SemaphoreType.DMA((130,)),
            pltpu.SemaphoreType.DMA((7,)),
        ],
        compiler_params=pltpu.CompilerParams(
            collective_id=0, has_side_effects=True, vmem_limit_bytes=63 * 2**20
        ),
        name="whole",
    )(ids, counts, cache, rope, weight, q, qr, og)


def shards(
    q_latent,
    q_rope,
    latent_cache,
    rope_keys,
    up_weight,
    out_grad,
    block_ids,
    block_counts,
    slab_offset,
):
    cg, rg, wg = finish(*run(
        block_ids[0],
        block_counts[0],
        latent_cache.reshape(12, 16, LAT),
        rope_keys[0].T,
        up_weight.reshape(128, HD),
        q_latent[0],
        q_rope[0],
        out_grad[0],
    ))
    return cg.reshape(1, 192, LAT), rg.T[None], wg.reshape(4, 32, HD)


def solution(mesh):
    placed = (
        P("dp", "ctx", None),
        P("dp", "ctx", None),
        P("dp", "ctx", None),
        P("dp", "ctx", None),
        P("ctx", "dp", None),
        P("dp", "ctx", None),
        P("dp", "ctx", None),
        P("dp", "ctx"),
        P("dp"),
    )
    return jax.shard_map(
        shards,
        mesh=mesh,
        in_specs=placed,
        out_specs=(P("dp", "ctx", None), P("dp", "ctx", None), P("ctx", "dp", None)),
        check_vma=False,
    )
```

```python
import functools

import jax
import jax.numpy as jnp
from jax import lax
from jax.experimental import pallas as pl
from jax.experimental.pallas import tpu as pltpu
from jax.sharding import PartitionSpec as P

LAT = 512
ROPE = 64
HD = 128
BLK = 64
SEL = 4
SCALE = (HD + ROPE) ** (-0.5)
TILES = 14
HALF = TILES // 2
MESH = pl.DeviceIdType.MESH
BF = jnp.bfloat16
F32 = jnp.float32


def place():
    dp, ctx = lax.axis_index("dp"), lax.axis_index("ctx")
    core, y, x_lo = dp % 2, (dp // 2) % 4, dp // 8
    x_hi, z = ctx // 8, ctx % 8
    return x_hi * 2 + x_lo, y, z, core, x_hi


def device(x, y, z, core):
    return (((x % 2) * 4 + y) * 2 + core, (x // 2) * 8 + z)


class Links:
    def __init__(self, send, recv):
        x, y, z, core, _ = place()
        self.send, self.recv, self.count, self.started = send, recv, 0, []
        self.to = {
            "z": (device(x, y, (z + 1) % 8, core), device(x, y, (z + 7) % 8, core)),
            "y": (device(x, (y + 1) % 4, z, core), device(x, (y + 3) % 4, z, core)),
            "x": (device((x + 1) % 4, y, z, core), device((x + 3) % 4, y, z, core)),
            "far": (device((x + 2) % 4, y, z, core),),
            "core": (device(x, y, z, 1 - core),),
        }
        for n in range(1, 8):
            self.to["z", n] = (device(x, y, (z + n) % 8, core),)

    def barrier(self):
        sem = pltpu.get_barrier_semaphore()
        partners = [d for way, group in self.to.items() if way != "z" for d in group]
        for d in partners:
            pl.semaphore_signal(sem, inc=1, device_id=d, device_id_type=MESH)
        pl.semaphore_wait(sem, len(partners))

    def push(self, src, dst, way, side=0, start=True):
        i = self.count
        self.count += 1
        copy = pltpu.make_async_remote_copy(
            src_ref=src,
            dst_ref=dst,
            send_sem=self.send.at[i],
            recv_sem=self.recv.at[i],
            device_id=self.to[way][side],
            device_id_type=MESH,
        )
        if start:
            copy.start()
        self.started.append(copy)
        return copy

    def finish(self):
        for copy in self.started:
            copy.wait_send()


def arrive(copies):
    for copy in copies:
        copy.wait_recv()


NT = (((1,), (1,)), ((), ()))
NN = (((1,), (0,)), ((), ()))


def dot(a, b, dims):
    return lax.dot_general(a, b, dims, preferred_element_type=F32)


def lanes_of(c, width):
    return pl.ds(pl.multiple_of(c * width, width), width)


SPOTS = [(x_lo, y, core) for x_lo in range(2) for y in range(4) for core in range(2)]


def weight_at(part, xh, x_lo, y, core, z):
    return (core, y, 2 * xh + x_lo, z, slice(64 * part, 64 * part + 64))


def grad_at(part, xh, x_lo, y, core, z):
    xx = 2 * xh + x_lo
    return (0, core, y, xx, z) if part == 0 else (1, core, xx, y, z)


def grads_of_pair(og, i, xh, part):
    low = og[:, lanes_of((xh * 8 + i) * 2 + part, 2 * HD)]
    zero = jnp.zeros((64, HD), BF)
    rows = []
    for b in range(2):
        first, second = low[64 * b : 64 * b + 64, :HD], low[64 * b : 64 * b + 64, HD:]
        rows.append(jnp.concatenate([first, zero], axis=1))
        rows.append(jnp.concatenate([zero, second], axis=1))
    return jnp.concatenate(rows, axis=0)


def queries(q, i, b):
    parts = []
    for xh in range(2):
        block = q[64 * b : 64 * b + 64, lanes_of(xh * 8 + i, 4 * LAT)]
        parts += [block[:, LAT * j : LAT * j + LAT] for j in range(4)]
    return jnp.concatenate(parts, axis=0)


def rotary(qr, i, b):
    low = lax.broadcasted_iota(jnp.int32, (64, 128), 1) < 64
    parts = []
    for xh in range(2):
        block = qr[64 * b : 64 * b + 64, lanes_of(xh * 8 + i, 4 * ROPE)].astype(F32)
        for j in range(4):
            slab = block[:, 128 * (j // 2) : 128 * (j // 2) + 128]
            slab = jnp.where(low, slab, 0.0) if j % 2 == 0 else jnp.where(low, 0.0, slab)
            parts.append(slab.astype(BF))
    return jnp.concatenate(parts, axis=0)


def scores(i, q, qr, k, bias, ph):
    for b in range(2):
        qs = jnp.concatenate([queries(q, i, b), rotary(qr, i, b)], axis=1)
        s = dot(k[b], qs, NT) * SCALE + jnp.concatenate([bias[b]] * 4, axis=1)
        e = jnp.exp(s - jnp.max(s, axis=0, keepdims=True))
        ph[i, b] = (e * (1.0 / jnp.sum(e, axis=0, keepdims=True))).astype(BF)


def outputs(i, og, kt, ph, d):
    outs = [dot(kt[b], ph[i, b], NN).astype(BF) for b in range(2)]
    for pair in range(4):
        xh, part = pair // 2, pair % 2
        both = jnp.concatenate([out[:, 128 * pair : 128 * pair + 128] for out in outs], axis=1)
        dw = dot(both, grads_of_pair(og, i, xh, part), NN).astype(BF)
        for n, spot in enumerate(SPOTS):
            rows = dw[32 * n : 32 * n + 32]
            d[grad_at(part, xh, *spot, i)] = jnp.concatenate([rows[:, :HD], rows[:, HD:]], axis=0)


def backward(i, q, qr, og, k, w, ph, dk, dr):
    backs = []
    for pair in range(4):
        xh, part = pair // 2, pair % 2
        pieces = [w[weight_at(part, xh, *spot, i)] for spot in SPOTS]
        weight = jnp.concatenate(
            [jnp.concatenate([p[:32], p[32:]], axis=1) for p in pieces], axis=0
        )
        backs.append(dot(grads_of_pair(og, i, xh, part), weight, NT).astype(BF))
    for b in range(2):
        back = jnp.concatenate([back[128 * b : 128 * b + 128] for back in backs], axis=0)
        dp = dot(k[b, :, :LAT], back, NT)
        half = ph[i, b]
        prob = half.astype(F32)
        weighted = prob * dp
        delta = jnp.sum(weighted, axis=0, keepdims=True)
        ds = ((weighted - prob * delta) * SCALE).astype(BF)
        dk[b] += dot(
            jnp.concatenate([half, ds], axis=1), jnp.concatenate([back, queries(q, i, b)], axis=0), NN
        )
        dr[b] += dot(ds, rotary(qr, i, b), NN)


def core_kernel(
    ids, counts, cache, rope, w_in, q_hbm, qr_hbm, og_hbm, cg, rg, wg,
    kc, g, d, core_in, q, qr, og, rope_v, k, kt, bias, ph, dk, dr, drp, cin, p1, p2, q1, q2, zin,
    send, recv, lsem,
):
    x, y, z, core, xh = place()
    links = Links(send, recv)
    mine = (y, x)

    def own(n):
        return xh * 8 + (z + n + 8) % 8

    def oth(n):
        return (1 - xh) * 8 + (z + n + 8) % 8

    def upper(side):
        return pl.ds(HALF * side, HALF)

    first = [
        pltpu.make_async_copy(cache, kc.at[own(0), pl.ds(0, 12)], lsem.at[0]),
        pltpu.make_async_copy(rope, rope_v, lsem.at[1]),
        pltpu.make_async_copy(w_in, g.at[core, y, x, z], lsem.at[2]),
    ]
    loads = [
        pltpu.make_async_copy(qr_hbm, qr, lsem.at[4]),
        pltpu.make_async_copy(og_hbm, og, lsem.at[5]),
        pltpu.make_async_copy(q_hbm, q, lsem.at[6]),
    ]
    for copy in first:
        copy.start()
    links.barrier()
    for copy in first:
        copy.wait()
    flipped = jnp.concatenate([rope_v[...].astype(F32), jnp.zeros((ROPE, 64), F32)], axis=1)
    flipped = jnp.concatenate([flipped, jnp.zeros((128 - ROPE, 256), F32)], axis=0).T
    packed = [flipped[32 * i : 32 * i + 32, :ROPE].astype(BF) for i in range(6)]
    packed = jnp.concatenate(packed + [jnp.zeros((32, 128), BF)], axis=1)
    kc[own(0), 12] = packed[:16]
    kc[own(0), 13] = packed[16:]

    def ring_x(s):
        out = []
        for side, sign in ((0, 1), (1, -1)):
            if s == 1:
                ref = g.at[core, y, x]
            else:
                ref = g.at[core, y, (x - sign + 4) % 4, pl.ds(4 * side, 4)]
            out.append(links.push(ref, ref, "x", side))
        return out

    def ring_y1(n):
        ref = g.at[core, y, (x + n + 4) % 4]
        return [links.push(ref, ref, "y", side) for side in (0, 1)]

    def ring_y2(n, start=True):
        out = []
        for side, sign in ((0, 1), (1, -1)):
            ref = g.at[core, (y - sign + 4) % 4, (x + n + 4) % 4, pl.ds(4 * side, 4)]
            out.append(links.push(ref, ref, "y", side, start))
        return out

    shared = []

    def share(n, start=True):
        ref = g.at[core, (y + n) % 4]
        shared.append(links.push(ref, ref, "core", 0, start))
        return shared[-1]

    def share_far(n):
        ref = g.at[core, (y + 2) % 4, (x + n) % 4]
        shared.append(links.push(ref, ref, "core", 0, False))
        return shared[-1]

    def ring8(s):
        out = []
        for side, sign in ((0, 1), (1, -1)):
            ref = kc.at[own(-sign * (s - 1))]
            if s == 4:
                ref = ref.at[upper(side)]
            out.append(links.push(ref, ref, "z", side))
        return out

    def push_block(o, way, side=0, rows=None):
        ref = kc.at[o]
        if rows is not None:
            ref = ref.at[rows]
        return links.push(ref, ref, way, side)

    weights = g.at[core, y, x, z]
    c = ring8(1)
    cross0 = push_block(own(0), "far")
    wz = [links.push(weights, weights, ("z", n)) for n in (4, 3, 5, 2, 6, 1, 7)]
    arrive(c)
    c = ring8(2)
    for copy in loads:
        copy.start()
    arrive(wz)
    ya = ring_y1(0)
    wx = ring_x(1)
    arrive([cross0])
    near = [push_block(oth(0), "z", 0), push_block(oth(0), "z", 1)]
    arrive(c)
    c = ring8(3)
    cross2 = [push_block(own(2), "far"), push_block(own(-2), "far")]
    arrive(ya)
    ya2 = ring_y2(0)
    arrive(wx)
    wx = ring_x(2)
    yb = ring_y1(1) + ring_y1(-1)
    arrive(c)
    c = ring8(4)
    arrive(c)
    cross4 = push_block(own(4), "far")
    arrive(wx)
    yc = ring_y1(2)
    share(0)
    arrive(cross2)
    third = [push_block(oth(-2), "z", 0), push_block(oth(2), "z", 1)]
    arrive(yb)
    yb2 = ring_y2(1) + ring_y2(-1)
    row = lax.broadcasted_iota(jnp.int32, (256, 128), 0)
    col = lax.broadcasted_iota(jnp.int32, (256, 128), 1)
    for n in range(2):
        slot = row // 64
        causal = jnp.where(row % 64 <= col % 64, 0.0, -1e30).astype(F32)
        listed = jnp.where(slot < counts[n], 0.0, -1e30).astype(F32)
        bias[n] = jnp.where(slot == 0, causal, listed)
    dk[...] = jnp.zeros_like(dk)
    dr[...] = jnp.zeros_like(dr)
    for copy in loads:
        copy.wait()
    arrive(near)
    arrive([cross4])
    arrive(third)

    for n in range(2):
        for j in range(SEL):
            owner, part = lax.div(ids[n, j], 3), lax.rem(ids[n, j], 3)
            for r in range(4):
                k[n, 64 * j + 16 * r : 64 * j + 16 * r + 16, :LAT] = kc[owner, 4 * part + r]
            for r in range(2):
                packs = kc[owner, 12 + r].astype(F32)
                pack = packs[:, 256:384]
                pack = jnp.where(part == 0, packs[:, 0:128], pack)
                pack = jnp.where(part == 1, packs[:, 128:256], pack)
                low, high = pack[:, :64].astype(BF), pack[:, 64:].astype(BF)
                row = 64 * j + 16 * r
                k[n, row : row + 16, LAT:] = jnp.concatenate([low, low], axis=1)
                k[n, row + 32 : row + 48, LAT:] = jnp.concatenate([high, high], axis=1)
        kt[n] = k[n, :, :LAT].T

    first_swap = links.count
    links.count += 8

    def swap(i):
        return pltpu.make_async_remote_copy(
            src_ref=d.at[:, 1 - core, :, :, i],
            dst_ref=core_in.at[:, :, :, i],
            send_sem=send.at[first_swap + i],
            recv_sem=recv.at[first_swap + i],
            device_id=links.to["core"][0],
            device_id_type=MESH,
        )

    def add(dst, *srcs):
        total = dst[...].astype(F32)
        for src in srcs:
            total = total + src[...].astype(F32)
        dst[...] = total.astype(BF)

    def swap_add(i):
        swap(i).wait_recv()
        for part in (0, 1):
            for n in range(4):
                add(d.at[part, core, n, :, i], core_in.at[part, n, :, i])

    def p_send1(h, start=True):
        out = []
        for part, way in ((0, "y"), (1, "x")):
            for side in (0, 1):
                ref = d.at[part, core, (mine[part] + 2) % 4, pl.ds(2 * side, 2), pl.ds(4 * h, 4)]
                out.append(links.push(ref, p1.at[h, part, side], way, side, start))
        return out

    def p_add1(h):
        for part in (0, 1):
            for side, sign in ((0, 1), (1, -1)):
                o = (mine[part] + sign + 4) % 4
                for n in range(2):
                    add(d.at[part, core, o, 2 * side + n, pl.ds(4 * h, 4)], p1.at[h, part, side, n])

    def p_send2(h, start=True):
        out = []
        for part, way in ((0, "y"), (1, "x")):
            for side, sign in ((0, 1), (1, -1)):
                ref = d.at[part, core, (mine[part] + sign + 4) % 4, :, pl.ds(4 * h, 4)]
                out.append(links.push(ref, p2.at[h, part, side], way, side, start))
        return out

    def p_add2(h):
        for part in (0, 1):
            for n in range(4):
                ref = d.at[part, core, mine[part], n, pl.ds(4 * h, 4)]
                add(ref, p2.at[h, part, 0, n], p2.at[h, part, 1, n])

    def q_send1():
        out = []
        for part, way in ((0, "x"), (1, "y")):
            o = (mine[1 - part] + 2) % 4
            for side in (0, 1):
                rows = pl.ds(4 * side, 4)
                out.append(links.push(d.at[part, core, mine[part], o, rows], q1.at[part, side], way, side))
        return out

    def q_add1():
        for part in (0, 1):
            for side, sign in ((0, 1), (1, -1)):
                o = (mine[1 - part] + sign + 4) % 4
                add(d.at[part, core, mine[part], o, pl.ds(4 * side, 4)], q1.at[part, side])

    def q_send2():
        out = []
        for part, way in ((0, "x"), (1, "y")):
            for side, sign in ((0, 1), (1, -1)):
                o = (mine[1 - part] + sign + 4) % 4
                out.append(links.push(d.at[part, core, mine[part], o], q2.at[part, side], way, side))
        return out

    def q_add2():
        for part in (0, 1):
            add(d.at[part, core, mine[part], mine[1 - part]], q2.at[part, 0], q2.at[part, 1])

    def total_of(part):
        total = d[part, core, mine[part], mine[1 - part], z].astype(F32)
        for n in range(7):
            total = total + zin[part, n].astype(F32)
        return total

    yc2 = ring_y2(2, False)
    late = [share(1, False), share(3, False)] + [share_far(n) for n in (0, 1, 3, 2)]
    pa1 = p_send1(0, False)

    scores(0, q, qr, k, bias, ph)

    @pl.loop(1, 8)
    def _(i):
        scores(i, q, qr, k, bias, ph)
        outputs(i - 1, og, kt, ph, d)
        swap(i - 1).start()

        @pl.when(i > 1)
        def _():
            swap_add(i - 2)

        @pl.when(i == 1)
        def _():
            arrive(yc)
            for copy in yc2:
                copy.start()
            arrive(ya2)
            for copy in late[:3]:
                copy.start()

        @pl.when(i == 5)
        def _():
            for copy in pa1:
                copy.start()

        @pl.when(i == 4)
        def _():
            arrive(yb2)
            late[3].start()
            late[4].start()

    outputs(7, og, kt, ph, d)
    swap(7).start()
    swap_add(6)
    arrive(yc2)
    late[5].start()
    swap_add(7)
    pb1 = p_send1(1)
    arrive(shared)
    pa2, pb2 = p_send2(0, False), p_send2(1, False)

    @pl.loop(0, 8)
    def _(i):
        backward(i, q, qr, og, k, g, ph, dk, dr)

        @pl.when(i == 0)
        def _():
            arrive(pa1)
            p_add1(0)
            for copy in pa2:
                copy.start()

        @pl.when(i == 2)
        def _():
            arrive(pb1)
            p_add1(1)
            for copy in pb2:
                copy.start()

        @pl.when(i == 6)
        def _():
            arrive(pa2)
            p_add2(0)

    links.finish()
    links.started = []
    for n in range(2):
        for j in range(SEL):
            fold = dr[n, 64 * j : 64 * j + 64, :]
            fold = fold[:, :64] + fold[:, 64:]
            drp[SEL * n + j] = jnp.concatenate([fold[:32], fold[32:]], axis=1)

    def fill(o):
        hits = [
            [jnp.where(ids[n, j] == o * 3 + part, 1.0, 0.0).astype(F32) for n in range(2) for j in range(SEL)]
            for part in range(3)
        ]
        packs = []
        for part in range(3):
            pack = jnp.zeros((32, 128), F32)
            for n in range(2 * SEL):
                pack = pack + hits[part][n] * drp[n]
            packs.append(pack.astype(BF))
            for r in range(4):
                total = jnp.zeros((16, LAT), F32)
                for n in range(2 * SEL):
                    low = 64 * (n % SEL) + 16 * r
                    total = total + hits[part][n] * dk[n // SEL, low : low + 16, :]
                kc[o, 4 * part + r] = total.astype(BF)
        packs = jnp.concatenate(packs + [jnp.zeros((32, 128), BF)], axis=1)
        kc[o, 12] = packs[:16]
        kc[o, 13] = packs[16:]

    def away(o, slot, way, side=0, rows=None):
        src, dst = kc.at[o], cin.at[slot]
        if rows is not None:
            src, dst = src.at[rows], dst.at[rows]
        return links.push(src, dst, way, side)

    def take(o, slots, rows=slice(None)):
        total = kc[o, rows].astype(F32)
        for slot in slots:
            total = total + cin[slot, rows].astype(F32)
        kc[o, rows] = total.astype(BF)

    lower, higher = slice(0, HALF), slice(HALF, TILES)
    fill(oth(4))
    cross4 = away(oth(4), 0, "far")
    fill(oth(3))
    fill(oth(-3))
    third = [away(oth(3), 1, "z", 0), away(oth(-3), 2, "z", 1)]
    fill(oth(2))
    fill(oth(-2))
    fill(own(4))
    arrive(pb2)
    p_add2(1)
    w = q_send1()
    arrive(third)
    take(oth(2), [1])
    take(oth(-2), [2])
    cross2 = [away(oth(2), 3, "far"), away(oth(-2), 4, "far")]
    arrive([cross4])
    take(own(4), [0])
    c = [away(own(4), 5, "z", 0, upper(0)), away(own(4), 6, "z", 1, upper(1))]
    fill(own(3))
    fill(own(-3))
    arrive(c)
    take(own(3), [5], lower)
    take(own(-3), [6], higher)
    c = [away(own(3), 7, "z", 0), away(own(-3), 8, "z", 1)]
    arrive(w)
    q_add1()
    w = q_send2()
    fill(oth(1))
    fill(oth(-1))
    near = [away(oth(1), 9, "z", 0, upper(1)), away(oth(-1), 10, "z", 1, upper(0))]
    cross1 = [away(oth(1), 11, "far", 0, upper(0)), away(oth(-1), 12, "far", 0, upper(1))]
    fill(own(2))
    fill(own(-2))
    fill(oth(0))
    arrive(c)
    arrive(cross2)
    take(own(2), [7, 3])
    take(own(-2), [8, 4])
    c = [away(own(2), 13, "z", 0), away(own(-2), 14, "z", 1)]
    arrive(near)
    take(oth(0), [9], higher)
    take(oth(0), [10], lower)
    cross0 = away(oth(0), 15, "far")
    arrive(w)
    q_add2()
    w = [
        links.push(
            d.at[part, core, mine[part], mine[1 - part], (z + n) % 8], zin.at[part, n - 1], ("z", n)
        )
        for n in (4, 3, 5, 2, 6, 1, 7)
        for part in (0, 1)
    ]
    fill(own(1))
    fill(own(-1))
    fill(own(0))
    arrive(cross1)
    take(own(1), [11], lower)
    take(own(-1), [12], higher)
    arrive(c)
    take(own(1), [13])
    take(own(-1), [14])
    c = [away(own(1), 16, "z", 0), away(own(-1), 17, "z", 1)]
    arrive(w)
    wg[0:64, :] = total_of(0)
    wg[64:128, :] = total_of(1)
    arrive([cross0])
    arrive(c)
    total = kc[own(0)].astype(F32)
    for slot in (15, 16, 17):
        total = total + cin[slot].astype(F32)
    cg[...] = total[0:12].astype(BF)
    pack = total[12:14].reshape(32, LAT)
    rows = [pack[:, 64 * i : 64 * i + 64] for i in range(6)] + [jnp.zeros((64, ROPE), F32)]
    flipped = jnp.concatenate(rows, axis=0)
    flipped = jnp.concatenate([flipped, jnp.zeros((256, 128 - ROPE), F32)], axis=1).T
    rg[...] = flipped[:ROPE, :192].astype(BF)
    links.finish()

    @pl.loop(0, 8)
    def _(i):
        swap(i).wait_send()


def finish_kernel(cg, rg, wg, cg_out, rg_out, wg_out):
    cg_out[...] = cg[...]
    rg_out[...] = rg[...]
    wg_out[...] = wg[...]


def finish(*arrays):
    return pl.pallas_call(
        finish_kernel,
        out_shape=tuple(jax.ShapeDtypeStruct(a.shape, a.dtype) for a in arrays),
        in_specs=[pl.BlockSpec(memory_space=pltpu.VMEM)] * 3,
        out_specs=(pl.BlockSpec(memory_space=pltpu.VMEM),) * 3,
        name="finish",
    )(*arrays)


def run(ids, counts, cache, rope, weight, q, qr, og):
    return pl.pallas_call(
        core_kernel,
        out_shape=(
            jax.ShapeDtypeStruct((12, 16, LAT), BF),
            jax.ShapeDtypeStruct((ROPE, 192), BF),
            jax.ShapeDtypeStruct((128, HD), F32),
        ),
        in_specs=[pl.BlockSpec(memory_space=pltpu.SMEM)] * 2 + [pl.BlockSpec(memory_space=pl.ANY)] * 6,
        out_specs=(pl.BlockSpec(memory_space=pltpu.VMEM),) * 3,
        scratch_shapes=[
            pltpu.VMEM((16, TILES, 16, LAT), BF),
            pltpu.VMEM((2, 4, 4, 8, 128, HD), BF),
            pltpu.VMEM((2, 2, 4, 4, 8, 64, HD), BF),
            pltpu.VMEM((2, 4, 4, 8, 64, HD), BF),
            pltpu.VMEM((128, 64 * LAT), BF),
            pltpu.VMEM((128, 64 * ROPE), BF),
            pltpu.VMEM((128, 64 * HD), BF),
            pltpu.VMEM((ROPE, 192), BF),
            pltpu.VMEM((2, 256, LAT + 128), BF),
            pltpu.VMEM((2, LAT, 256), BF),
            pltpu.VMEM((2, 256, 128), F32),
            pltpu.VMEM((8, 2, 256, 512), BF),
            pltpu.VMEM((2, 256, LAT), F32),
            pltpu.VMEM((2, 256, 128), F32),
            pltpu.VMEM((2 * SEL, 32, 128), F32),
            pltpu.VMEM((18, TILES, 16, LAT), BF),
            pltpu.VMEM((2, 2, 2, 2, 4, 64, HD), BF),
            pltpu.VMEM((2, 2, 2, 4, 4, 64, HD), BF),
            pltpu.VMEM((2, 2, 4, 64, HD), BF),
            pltpu.VMEM((2, 2, 8, 64, HD), BF),
            pltpu.VMEM((2, 7, 64, HD), BF),
            pltpu.SemaphoreType.DMA((130,)),
            pltpu.SemaphoreType.DMA((130,)),
            pltpu.SemaphoreType.DMA((7,)),
        ],
        compiler_params=pltpu.CompilerParams(
            collective_id=0, has_side_effects=True, vmem_limit_bytes=63 * 2**20
        ),
        name="whole",
    )(ids, counts, cache, rope, weight, q, qr, og)


def shards(
    q_latent,
    q_rope,
    latent_cache,
    rope_keys,
    up_weight,
    out_grad,
    block_ids,
    block_counts,
    slab_offset,
):
    cg, rg, wg = finish(*run(
        block_ids[0],
        block_counts[0],
        latent_cache.reshape(12, 16, LAT),
        rope_keys[0].T,
        up_weight.reshape(128, HD),
        q_latent[0],
        q_rope[0],
        out_grad[0],
    ))
    return cg.reshape(1, 192, LAT), rg.T[None], wg.reshape(4, 32, HD)


def solution(mesh):
    placed = (
        P("dp", "ctx", None),
        P("dp", "ctx", None),
        P("dp", "ctx", None),
        P("dp", "ctx", None),
        P("ctx", "dp", None),
        P("dp", "ctx", None),
        P("dp", "ctx", None),
        P("dp", "ctx"),
        P("dp"),
    )
    return jax.shard_map(
        shards,
        mesh=mesh,
        in_specs=placed,
        out_specs=(P("dp", "ctx", None), P("dp", "ctx", None), P("ctx", "dp", None)),
        check_vma=False,
    )
```

```python
import functools

import jax
import jax.numpy as jnp
from jax import lax
from jax.experimental import pallas as pl
from jax.experimental.pallas import tpu as pltpu
from jax.sharding import PartitionSpec as P

LAT = 512
ROPE = 64
HD = 128
BLK = 64
SEL = 4
SCALE = (HD + ROPE) ** (-0.5)
TILES = 14
HALF = TILES // 2
MESH = pl.DeviceIdType.MESH
BF = jnp.bfloat16
F32 = jnp.float32


def place():
    dp, ctx = lax.axis_index("dp"), lax.axis_index("ctx")
    core, y, x_lo = dp % 2, (dp // 2) % 4, dp // 8
    x_hi, z = ctx // 8, ctx % 8
    return x_hi * 2 + x_lo, y, z, core, x_hi


def device(x, y, z, core):
    return (((x % 2) * 4 + y) * 2 + core, (x // 2) * 8 + z)


class Links:
    def __init__(self, send, recv):
        x, y, z, core, _ = place()
        self.send, self.recv, self.count, self.started = send, recv, 0, []
        self.to = {
            "z": (device(x, y, (z + 1) % 8, core), device(x, y, (z + 7) % 8, core)),
            "y": (device(x, (y + 1) % 4, z, core), device(x, (y + 3) % 4, z, core)),
            "x": (device((x + 1) % 4, y, z, core), device((x + 3) % 4, y, z, core)),
            "far": (device((x + 2) % 4, y, z, core),),
            "core": (device(x, y, z, 1 - core),),
        }
        for n in range(1, 8):
            self.to["z", n] = (device(x, y, (z + n) % 8, core),)

    def barrier(self):
        sem = pltpu.get_barrier_semaphore()
        partners = [d for way, group in self.to.items() if way != "z" for d in group]
        for d in partners:
            pl.semaphore_signal(sem, inc=1, device_id=d, device_id_type=MESH)
        pl.semaphore_wait(sem, len(partners))

    def push(self, src, dst, way, side=0, start=True):
        i = self.count
        self.count += 1
        copy = pltpu.make_async_remote_copy(
            src_ref=src,
            dst_ref=dst,
            send_sem=self.send.at[i],
            recv_sem=self.recv.at[i],
            device_id=self.to[way][side],
            device_id_type=MESH,
        )
        if start:
            copy.start()
        self.started.append(copy)
        return copy

    def finish(self):
        for copy in self.started:
            copy.wait_send()


def arrive(copies):
    for copy in copies:
        copy.wait_recv()


NT = (((1,), (1,)), ((), ()))
NN = (((1,), (0,)), ((), ()))


def dot(a, b, dims):
    return lax.dot_general(a, b, dims, preferred_element_type=F32)


def lanes_of(c, width):
    return pl.ds(pl.multiple_of(c * width, width), width)


SPOTS = [(x_lo, y, core) for x_lo in range(2) for y in range(4) for core in range(2)]


def weight_at(part, xh, x_lo, y, core, z):
    return (core, y, 2 * xh + x_lo, z, slice(64 * part, 64 * part + 64))


def grad_at(part, xh, x_lo, y, core, z):
    xx = 2 * xh + x_lo
    return (0, core, y, xx, z) if part == 0 else (1, core, xx, y, z)


def grads_of_pair(og, i, xh, part):
    low = og[:, lanes_of((xh * 8 + i) * 2 + part, 2 * HD)]
    zero = jnp.zeros((64, HD), BF)
    rows = []
    for b in range(2):
        first, second = low[64 * b : 64 * b + 64, :HD], low[64 * b : 64 * b + 64, HD:]
        rows.append(jnp.concatenate([first, zero], axis=1))
        rows.append(jnp.concatenate([zero, second], axis=1))
    return jnp.concatenate(rows, axis=0)


def queries(q, i, b):
    parts = []
    for xh in range(2):
        block = q[64 * b : 64 * b + 64, lanes_of(xh * 8 + i, 4 * LAT)]
        parts += [block[:, LAT * j : LAT * j + LAT] for j in range(4)]
    return jnp.concatenate(parts, axis=0)


def rotary(qr, i, b):
    low = lax.broadcasted_iota(jnp.int32, (64, 128), 1) < 64
    parts = []
    for xh in range(2):
        block = qr[64 * b : 64 * b + 64, lanes_of(xh * 8 + i, 4 * ROPE)].astype(F32)
        for j in range(4):
            slab = block[:, 128 * (j // 2) : 128 * (j // 2) + 128]
            slab = jnp.where(low, slab, 0.0) if j % 2 == 0 else jnp.where(low, 0.0, slab)
            parts.append(slab.astype(BF))
    return jnp.concatenate(parts, axis=0)


def scores(i, q, qr, k, bias, ph):
    for b in range(2):
        qs = jnp.concatenate([queries(q, i, b), rotary(qr, i, b)], axis=1)
        s = dot(k[b], qs, NT) * SCALE + jnp.concatenate([bias[b]] * 4, axis=1)
        e = jnp.exp(s - jnp.max(s, axis=0, keepdims=True))
        ph[i, b] = (e * (1.0 / jnp.sum(e, axis=0, keepdims=True))).astype(BF)


def outputs(i, og, kt, ph, d):
    outs = [dot(kt[b], ph[i, b], NN).astype(BF) for b in range(2)]
    for pair in range(4):
        xh, part = pair // 2, pair % 2
        both = jnp.concatenate([out[:, 128 * pair : 128 * pair + 128] for out in outs], axis=1)
        dw = dot(both, grads_of_pair(og, i, xh, part), NN).astype(BF)
        for n, spot in enumerate(SPOTS):
            rows = dw[32 * n : 32 * n + 32]
            d[grad_at(part, xh, *spot, i)] = jnp.concatenate([rows[:, :HD], rows[:, HD:]], axis=0)


def backward(i, q, qr, og, k, w, ph, dk, dr):
    backs = []
    for pair in range(4):
        xh, part = pair // 2, pair % 2
        pieces = [w[weight_at(part, xh, *spot, i)] for spot in SPOTS]
        weight = jnp.concatenate(
            [jnp.concatenate([p[:32], p[32:]], axis=1) for p in pieces], axis=0
        )
        backs.append(dot(grads_of_pair(og, i, xh, part), weight, NT).astype(BF))
    for b in range(2):
        back = jnp.concatenate([back[128 * b : 128 * b + 128] for back in backs], axis=0)
        dp = dot(k[b, :, :LAT], back, NT)
        half = ph[i, b]
        prob = half.astype(F32)
        weighted = prob * dp
        delta = jnp.sum(weighted, axis=0, keepdims=True)
        ds = ((weighted - prob * delta) * SCALE).astype(BF)
        dk[b] += dot(
            jnp.concatenate([half, ds], axis=1), jnp.concatenate([back, queries(q, i, b)], axis=0), NN
        )
        dr[b] += dot(ds, rotary(qr, i, b), NN)


def core_kernel(
    ids, counts, cache, rope, w_in, q_hbm, qr_hbm, og_hbm, cg, rg, wg,
    kc, g, d, core_in, q, qr, og, rope_v, k, kt, bias, ph, dk, dr, drp, cin, p1, p2, q1, q2, zin,
    send, recv, lsem,
):
    x, y, z, core, xh = place()
    links = Links(send, recv)
    mine = (y, x)

    def own(n):
        return xh * 8 + (z + n + 8) % 8

    def oth(n):
        return (1 - xh) * 8 + (z + n + 8) % 8

    def upper(side):
        return pl.ds(HALF * side, HALF)

    first = [
        pltpu.make_async_copy(cache, kc.at[own(0), pl.ds(0, 12)], lsem.at[0]),
        pltpu.make_async_copy(rope, rope_v, lsem.at[1]),
        pltpu.make_async_copy(w_in, g.at[core, y, x, z], lsem.at[2]),
    ]
    loads = [
        pltpu.make_async_copy(qr_hbm, qr, lsem.at[4]),
        pltpu.make_async_copy(og_hbm, og, lsem.at[5]),
        pltpu.make_async_copy(q_hbm, q, lsem.at[6]),
    ]
    for copy in first:
        copy.start()
    links.barrier()
    for copy in first:
        copy.wait()
    flipped = jnp.concatenate([rope_v[...].astype(F32), jnp.zeros((ROPE, 64), F32)], axis=1)
    flipped = jnp.concatenate([flipped, jnp.zeros((128 - ROPE, 256), F32)], axis=0).T
    packed = [flipped[32 * i : 32 * i + 32, :ROPE].astype(BF) for i in range(6)]
    packed = jnp.concatenate(packed + [jnp.zeros((32, 128), BF)], axis=1)
    kc[own(0), 12] = packed[:16]
    kc[own(0), 13] = packed[16:]

    def ring_x(s):
        out = []
        for side, sign in ((0, 1), (1, -1)):
            if s == 1:
                ref = g.at[core, y, x]
            else:
                ref = g.at[core, y, (x - sign + 4) % 4, pl.ds(4 * side, 4)]
            out.append(links.push(ref, ref, "x", side))
        return out

    def ring_y1(n):
        ref = g.at[core, y, (x + n + 4) % 4]
        return [links.push(ref, ref, "y", side) for side in (0, 1)]

    def ring_y2(n, start=True):
        out = []
        for side, sign in ((0, 1), (1, -1)):
            ref = g.at[core, (y - sign + 4) % 4, (x + n + 4) % 4, pl.ds(4 * side, 4)]
            out.append(links.push(ref, ref, "y", side, start))
        return out

    shared = []

    def share(n, start=True):
        ref = g.at[core, (y + n) % 4]
        shared.append(links.push(ref, ref, "core", 0, start))
        return shared[-1]

    def share_far(n):
        ref = g.at[core, (y + 2) % 4, (x + n) % 4]
        shared.append(links.push(ref, ref, "core", 0, False))
        return shared[-1]

    kept = []

    def ring8(s):
        out = []
        for side, sign in ((0, 1), (1, -1)):
            rows = upper(side) if s == 4 else None
            out.append(push_block(own(-sign * (s - 1)), "z", side, rows))
        return out

    def push_block(o, way, side=0, rows=None):
        ref = kc.at[o]
        if rows is not None:
            ref = ref.at[rows]
        kept.append(links.push(ref, ref, way, side))
        return kept[-1]

    weights = g.at[core, y, x, z]
    c = ring8(1)
    cross0 = push_block(own(0), "far")
    wz = [links.push(weights, weights, ("z", n)) for n in (4, 3, 5, 2, 6, 1, 7)]
    arrive(c)
    c = ring8(2)
    for copy in loads:
        copy.start()
    arrive(wz)
    ya = ring_y1(0)
    wx = ring_x(1)
    arrive([cross0])
    near = [push_block(oth(0), "z", 0), push_block(oth(0), "z", 1)]
    arrive(c)
    c = ring8(3)
    cross2 = [push_block(own(2), "far"), push_block(own(-2), "far")]
    arrive(ya)
    ya2 = ring_y2(0)
    arrive(wx)
    wx = ring_x(2)
    yb = ring_y1(1) + ring_y1(-1)
    arrive(c)
    c = ring8(4)
    arrive(c)
    cross4 = push_block(own(4), "far")
    arrive(wx)
    yc = ring_y1(2)
    share(0)
    arrive(cross2)
    third = [push_block(oth(-2), "z", 0), push_block(oth(2), "z", 1)]
    arrive(yb)
    yb2 = ring_y2(1) + ring_y2(-1)
    row = lax.broadcasted_iota(jnp.int32, (256, 128), 0)
    col = lax.broadcasted_iota(jnp.int32, (256, 128), 1)
    for n in range(2):
        slot = row // 64
        causal = jnp.where(row % 64 <= col % 64, 0.0, -1e30).astype(F32)
        listed = jnp.where(slot < counts[n], 0.0, -1e30).astype(F32)
        bias[n] = jnp.where(slot == 0, causal, listed)
    dk[...] = jnp.zeros_like(dk)
    dr[...] = jnp.zeros_like(dr)
    for copy in loads:
        copy.wait()
    arrive(near)
    arrive([cross4])
    arrive(third)

    for n in range(2):
        for j in range(SEL):
            owner, part = lax.div(ids[n, j], 3), lax.rem(ids[n, j], 3)
            for r in range(4):
                k[n, 64 * j + 16 * r : 64 * j + 16 * r + 16, :LAT] = kc[owner, 4 * part + r]
            for r in range(2):
                packs = kc[owner, 12 + r].astype(F32)
                pack = packs[:, 256:384]
                pack = jnp.where(part == 0, packs[:, 0:128], pack)
                pack = jnp.where(part == 1, packs[:, 128:256], pack)
                low, high = pack[:, :64].astype(BF), pack[:, 64:].astype(BF)
                row = 64 * j + 16 * r
                k[n, row : row + 16, LAT:] = jnp.concatenate([low, low], axis=1)
                k[n, row + 32 : row + 48, LAT:] = jnp.concatenate([high, high], axis=1)
        kt[n] = k[n, :, :LAT].T

    first_swap = links.count
    links.count += 8

    def swap(i):
        return pltpu.make_async_remote_copy(
            src_ref=d.at[:, 1 - core, :, :, i],
            dst_ref=core_in.at[:, :, :, i],
            send_sem=send.at[first_swap + i],
            recv_sem=recv.at[first_swap + i],
            device_id=links.to["core"][0],
            device_id_type=MESH,
        )

    def add(dst, *srcs):
        total = dst[...].astype(F32)
        for src in srcs:
            total = total + src[...].astype(F32)
        dst[...] = total.astype(BF)

    def swap_add(i):
        swap(i).wait_recv()
        for part in (0, 1):
            for n in range(4):
                add(d.at[part, core, n, :, i], core_in.at[part, n, :, i])

    def p_send1(h, start=True):
        out = []
        for part, way in ((0, "y"), (1, "x")):
            for side in (0, 1):
                ref = d.at[part, core, (mine[part] + 2) % 4, pl.ds(2 * side, 2), pl.ds(4 * h, 4)]
                out.append(links.push(ref, p1.at[h, part, side], way, side, start))
        return out

    def p_add1(h):
        for part in (0, 1):
            for side, sign in ((0, 1), (1, -1)):
                o = (mine[part] + sign + 4) % 4
                for n in range(2):
                    add(d.at[part, core, o, 2 * side + n, pl.ds(4 * h, 4)], p1.at[h, part, side, n])

    def p_send2(h, start=True):
        out = []
        for part, way in ((0, "y"), (1, "x")):
            for side, sign in ((0, 1), (1, -1)):
                ref = d.at[part, core, (mine[part] + sign + 4) % 4, :, pl.ds(4 * h, 4)]
                out.append(links.push(ref, p2.at[h, part, side], way, side, start))
        return out

    def p_add2(h):
        for part in (0, 1):
            for n in range(4):
                ref = d.at[part, core, mine[part], n, pl.ds(4 * h, 4)]
                add(ref, p2.at[h, part, 0, n], p2.at[h, part, 1, n])

    def q_send1():
        out = []
        for part, way in ((0, "x"), (1, "y")):
            o = (mine[1 - part] + 2) % 4
            for side in (0, 1):
                rows = pl.ds(4 * side, 4)
                out.append(links.push(d.at[part, core, mine[part], o, rows], q1.at[part, side], way, side))
        return out

    def q_add1():
        for part in (0, 1):
            for side, sign in ((0, 1), (1, -1)):
                o = (mine[1 - part] + sign + 4) % 4
                add(d.at[part, core, mine[part], o, pl.ds(4 * side, 4)], q1.at[part, side])

    def q_send2():
        out = []
        for part, way in ((0, "x"), (1, "y")):
            for side, sign in ((0, 1), (1, -1)):
                o = (mine[1 - part] + sign + 4) % 4
                out.append(links.push(d.at[part, core, mine[part], o], q2.at[part, side], way, side))
        return out

    def q_add2():
        for part in (0, 1):
            add(d.at[part, core, mine[part], mine[1 - part]], q2.at[part, 0], q2.at[part, 1])

    def total_of(part):
        total = d[part, core, mine[part], mine[1 - part], z].astype(F32)
        for n in range(7):
            total = total + zin[part, n].astype(F32)
        return total

    yc2 = ring_y2(2, False)
    late = [share(1, False), share(3, False)] + [share_far(n) for n in (0, 1, 3, 2)]
    pa1 = p_send1(0, False)

    scores(0, q, qr, k, bias, ph)

    @pl.loop(1, 8)
    def _(i):
        scores(i, q, qr, k, bias, ph)
        outputs(i - 1, og, kt, ph, d)
        swap(i - 1).start()

        @pl.when(i > 1)
        def _():
            swap_add(i - 2)

        @pl.when(i == 1)
        def _():
            arrive(yc)
            for copy in yc2:
                copy.start()
            arrive(ya2)
            for copy in late[:3]:
                copy.start()

        @pl.when(i == 5)
        def _():
            for copy in pa1:
                copy.start()

        @pl.when(i == 4)
        def _():
            arrive(yb2)
            late[3].start()
            late[4].start()

    outputs(7, og, kt, ph, d)
    swap(7).start()
    swap_add(6)
    arrive(yc2)
    late[5].start()
    swap_add(7)
    pb1 = p_send1(1)
    arrive(shared)
    pa2, pb2 = p_send2(0, False), p_send2(1, False)

    @pl.loop(0, 8)
    def _(i):
        backward(i, q, qr, og, k, g, ph, dk, dr)

        @pl.when(i == 0)
        def _():
            arrive(pa1)
            p_add1(0)
            for copy in pa2:
                copy.start()

        @pl.when(i == 2)
        def _():
            arrive(pb1)
            p_add1(1)
            for copy in pb2:
                copy.start()

        @pl.when(i == 6)
        def _():
            arrive(pa2)
            p_add2(0)

    for copy in kept:
        copy.wait_send()
    links.started = [copy for copy in links.started if not any(copy is other for other in kept)]
    for n in range(2):
        for j in range(SEL):
            fold = dr[n, 64 * j : 64 * j + 64, :]
            fold = fold[:, :64] + fold[:, 64:]
            drp[SEL * n + j] = jnp.concatenate([fold[:32], fold[32:]], axis=1)

    def fill(o):
        hits = [
            [jnp.where(ids[n, j] == o * 3 + part, 1.0, 0.0).astype(F32) for n in range(2) for j in range(SEL)]
            for part in range(3)
        ]
        packs = []
        for part in range(3):
            pack = jnp.zeros((32, 128), F32)
            for n in range(2 * SEL):
                pack = pack + hits[part][n] * drp[n]
            packs.append(pack.astype(BF))
            for r in range(4):
                total = jnp.zeros((16, LAT), F32)
                for n in range(2 * SEL):
                    low = 64 * (n % SEL) + 16 * r
                    total = total + hits[part][n] * dk[n // SEL, low : low + 16, :]
                kc[o, 4 * part + r] = total.astype(BF)
        packs = jnp.concatenate(packs + [jnp.zeros((32, 128), BF)], axis=1)
        kc[o, 12] = packs[:16]
        kc[o, 13] = packs[16:]

    def away(o, slot, way, side=0, rows=None):
        src, dst = kc.at[o], cin.at[slot]
        if rows is not None:
            src, dst = src.at[rows], dst.at[rows]
        return links.push(src, dst, way, side)

    def take(o, slots, rows=slice(None)):
        total = kc[o, rows].astype(F32)
        for slot in slots:
            total = total + cin[slot, rows].astype(F32)
        kc[o, rows] = total.astype(BF)

    lower, higher = slice(0, HALF), slice(HALF, TILES)
    fill(oth(4))
    cross4 = away(oth(4), 0, "far")
    fill(oth(3))
    fill(oth(-3))
    third = [away(oth(3), 1, "z", 0), away(oth(-3), 2, "z", 1)]
    fill(oth(2))
    fill(oth(-2))
    fill(own(4))
    arrive(pb2)
    p_add2(1)
    w = q_send1()
    arrive(third)
    take(oth(2), [1])
    take(oth(-2), [2])
    cross2 = [away(oth(2), 3, "far"), away(oth(-2), 4, "far")]
    arrive([cross4])
    take(own(4), [0])
    c = [away(own(4), 5, "z", 0, upper(0)), away(own(4), 6, "z", 1, upper(1))]
    fill(own(3))
    fill(own(-3))
    arrive(c)
    take(own(3), [5], lower)
    take(own(-3), [6], higher)
    c = [away(own(3), 7, "z", 0), away(own(-3), 8, "z", 1)]
    arrive(w)
    q_add1()
    w = q_send2()
    fill(oth(1))
    fill(oth(-1))
    near = [away(oth(1), 9, "z", 0, upper(1)), away(oth(-1), 10, "z", 1, upper(0))]
    fill(own(2))
    fill(own(-2))
    fill(oth(0))
    cross1 = [away(oth(1), 11, "far", 0, upper(0)), away(oth(-1), 12, "far", 0, upper(1))]
    arrive(c)
    arrive(cross2)
    take(own(2), [7, 3])
    take(own(-2), [8, 4])
    c = [away(own(2), 13, "z", 0), away(own(-2), 14, "z", 1)]
    arrive(near)
    take(oth(0), [9], higher)
    take(oth(0), [10], lower)
    cross0 = away(oth(0), 15, "far")
    arrive(w)
    q_add2()
    w = [
        links.push(
            d.at[part, core, mine[part], mine[1 - part], (z + n) % 8], zin.at[part, n - 1], ("z", n)
        )
        for n in (4, 3, 5, 2, 6, 1, 7)
        for part in (0, 1)
    ]
    fill(own(1))
    fill(own(-1))
    fill(own(0))
    arrive(cross1)
    take(own(1), [11], lower)
    take(own(-1), [12], higher)
    arrive(c)
    take(own(1), [13])
    take(own(-1), [14])
    c = [away(own(1), 16, "z", 0), away(own(-1), 17, "z", 1)]
    arrive(w)
    wg[0:64, :] = total_of(0)
    wg[64:128, :] = total_of(1)
    arrive([cross0])
    arrive(c)
    total = kc[own(0)].astype(F32)
    for slot in (15, 16, 17):
        total = total + cin[slot].astype(F32)
    cg[...] = total[0:12].astype(BF)
    pack = total[12:14].reshape(32, LAT)
    rows = [pack[:, 64 * i : 64 * i + 64] for i in range(6)] + [jnp.zeros((64, ROPE), F32)]
    flipped = jnp.concatenate(rows, axis=0)
    flipped = jnp.concatenate([flipped, jnp.zeros((256, 128 - ROPE), F32)], axis=1).T
    rg[...] = flipped[:ROPE, :192].astype(BF)
    links.finish()

    @pl.loop(0, 8)
    def _(i):
        swap(i).wait_send()


def finish_kernel(cg, rg, wg, cg_out, rg_out, wg_out):
    cg_out[...] = cg[...]
    rg_out[...] = rg[...]
    wg_out[...] = wg[...]


def finish(*arrays):
    return pl.pallas_call(
        finish_kernel,
        out_shape=tuple(jax.ShapeDtypeStruct(a.shape, a.dtype) for a in arrays),
        in_specs=[pl.BlockSpec(memory_space=pltpu.VMEM)] * 3,
        out_specs=(pl.BlockSpec(memory_space=pltpu.VMEM),) * 3,
        name="finish",
    )(*arrays)


def run(ids, counts, cache, rope, weight, q, qr, og):
    return pl.pallas_call(
        core_kernel,
        out_shape=(
            jax.ShapeDtypeStruct((12, 16, LAT), BF),
            jax.ShapeDtypeStruct((ROPE, 192), BF),
            jax.ShapeDtypeStruct((128, HD), F32),
        ),
        in_specs=[pl.BlockSpec(memory_space=pltpu.SMEM)] * 2 + [pl.BlockSpec(memory_space=pl.ANY)] * 6,
        out_specs=(pl.BlockSpec(memory_space=pltpu.VMEM),) * 3,
        scratch_shapes=[
            pltpu.VMEM((16, TILES, 16, LAT), BF),
            pltpu.VMEM((2, 4, 4, 8, 128, HD), BF),
            pltpu.VMEM((2, 2, 4, 4, 8, 64, HD), BF),
            pltpu.VMEM((2, 4, 4, 8, 64, HD), BF),
            pltpu.VMEM((128, 64 * LAT), BF),
            pltpu.VMEM((128, 64 * ROPE), BF),
            pltpu.VMEM((128, 64 * HD), BF),
            pltpu.VMEM((ROPE, 192), BF),
            pltpu.VMEM((2, 256, LAT + 128), BF),
            pltpu.VMEM((2, LAT, 256), BF),
            pltpu.VMEM((2, 256, 128), F32),
            pltpu.VMEM((8, 2, 256, 512), BF),
            pltpu.VMEM((2, 256, LAT), F32),
            pltpu.VMEM((2, 256, 128), F32),
            pltpu.VMEM((2 * SEL, 32, 128), F32),
            pltpu.VMEM((18, TILES, 16, LAT), BF),
            pltpu.VMEM((2, 2, 2, 2, 4, 64, HD), BF),
            pltpu.VMEM((2, 2, 2, 4, 4, 64, HD), BF),
            pltpu.VMEM((2, 2, 4, 64, HD), BF),
            pltpu.VMEM((2, 2, 8, 64, HD), BF),
            pltpu.VMEM((2, 7, 64, HD), BF),
            pltpu.SemaphoreType.DMA((130,)),
            pltpu.SemaphoreType.DMA((130,)),
            pltpu.SemaphoreType.DMA((7,)),
        ],
        compiler_params=pltpu.CompilerParams(
            collective_id=0, has_side_effects=True, vmem_limit_bytes=63 * 2**20
        ),
        name="whole",
    )(ids, counts, cache, rope, weight, q, qr, og)


def shards(
    q_latent,
    q_rope,
    latent_cache,
    rope_keys,
    up_weight,
    out_grad,
    block_ids,
    block_counts,
    slab_offset,
):
    cg, rg, wg = finish(*run(
        block_ids[0],
        block_counts[0],
        latent_cache.reshape(12, 16, LAT),
        rope_keys[0].T,
        up_weight.reshape(128, HD),
        q_latent[0],
        q_rope[0],
        out_grad[0],
    ))
    return cg.reshape(1, 192, LAT), rg.T[None], wg.reshape(4, 32, HD)


def solution(mesh):
    placed = (
        P("dp", "ctx", None),
        P("dp", "ctx", None),
        P("dp", "ctx", None),
        P("dp", "ctx", None),
        P("ctx", "dp", None),
        P("dp", "ctx", None),
        P("dp", "ctx", None),
        P("dp", "ctx"),
        P("dp"),
    )
    return jax.shard_map(
        shards,
        mesh=mesh,
        in_specs=placed,
        out_specs=(P("dp", "ctx", None), P("dp", "ctx", None), P("ctx", "dp", None)),
        check_vma=False,
    )
```

```python
import functools

import jax
import jax.numpy as jnp
from jax import lax
from jax.experimental import pallas as pl
from jax.experimental.pallas import tpu as pltpu
from jax.sharding import PartitionSpec as P

LAT = 512
ROPE = 64
HD = 128
BLK = 64
SEL = 4
SCALE = (HD + ROPE) ** (-0.5)
TILES = 14
HALF = TILES // 2
MESH = pl.DeviceIdType.MESH
BF = jnp.bfloat16
F32 = jnp.float32


def place():
    dp, ctx = lax.axis_index("dp"), lax.axis_index("ctx")
    core, y, x_lo = dp % 2, (dp // 2) % 4, dp // 8
    x_hi, z = ctx // 8, ctx % 8
    return x_hi * 2 + x_lo, y, z, core, x_hi


def device(x, y, z, core):
    return (((x % 2) * 4 + y) * 2 + core, (x // 2) * 8 + z)


class Links:
    def __init__(self, send, recv):
        x, y, z, core, _ = place()
        self.send, self.recv, self.count, self.started = send, recv, 0, []
        self.to = {
            "z": (device(x, y, (z + 1) % 8, core), device(x, y, (z + 7) % 8, core)),
            "y": (device(x, (y + 1) % 4, z, core), device(x, (y + 3) % 4, z, core)),
            "x": (device((x + 1) % 4, y, z, core), device((x + 3) % 4, y, z, core)),
            "far": (device((x + 2) % 4, y, z, core),),
            "core": (device(x, y, z, 1 - core),),
        }
        for n in range(1, 8):
            self.to["z", n] = (device(x, y, (z + n) % 8, core),)

    def barrier(self):
        sem = pltpu.get_barrier_semaphore()
        partners = [d for way, group in self.to.items() if way != "z" for d in group]
        for d in partners:
            pl.semaphore_signal(sem, inc=1, device_id=d, device_id_type=MESH)
        pl.semaphore_wait(sem, len(partners))

    def push(self, src, dst, way, side=0, start=True):
        i = self.count
        self.count += 1
        copy = pltpu.make_async_remote_copy(
            src_ref=src,
            dst_ref=dst,
            send_sem=self.send.at[i],
            recv_sem=self.recv.at[i],
            device_id=self.to[way][side],
            device_id_type=MESH,
        )
        if start:
            copy.start()
        self.started.append(copy)
        return copy

    def finish(self):
        for copy in self.started:
            copy.wait_send()


def arrive(copies):
    for copy in copies:
        copy.wait_recv()


NT = (((1,), (1,)), ((), ()))
NN = (((1,), (0,)), ((), ()))


def dot(a, b, dims):
    return lax.dot_general(a, b, dims, preferred_element_type=F32)


def lanes_of(c, width):
    return pl.ds(pl.multiple_of(c * width, width), width)


SPOTS = [(x_lo, y, core) for x_lo in range(2) for y in range(4) for core in range(2)]


def weight_at(part, xh, x_lo, y, core, z):
    return (core, y, 2 * xh + x_lo, z, slice(64 * part, 64 * part + 64))


def grad_at(part, xh, x_lo, y, core, z):
    xx = 2 * xh + x_lo
    return (0, core, y, xx, z) if part == 0 else (1, core, xx, y, z)


def grads_of_pair(og, i, xh, part):
    low = og[:, lanes_of((xh * 8 + i) * 2 + part, 2 * HD)]
    zero = jnp.zeros((64, HD), BF)
    rows = []
    for b in range(2):
        first, second = low[64 * b : 64 * b + 64, :HD], low[64 * b : 64 * b + 64, HD:]
        rows.append(jnp.concatenate([first, zero], axis=1))
        rows.append(jnp.concatenate([zero, second], axis=1))
    return jnp.concatenate(rows, axis=0)


def queries(q, i, b):
    parts = []
    for xh in range(2):
        block = q[64 * b : 64 * b + 64, lanes_of(xh * 8 + i, 4 * LAT)]
        parts += [block[:, LAT * j : LAT * j + LAT] for j in range(4)]
    return jnp.concatenate(parts, axis=0)


def rotary(qr, i, b):
    low = lax.broadcasted_iota(jnp.int32, (64, 128), 1) < 64
    parts = []
    for xh in range(2):
        block = qr[64 * b : 64 * b + 64, lanes_of(xh * 8 + i, 4 * ROPE)].astype(F32)
        for j in range(4):
            slab = block[:, 128 * (j // 2) : 128 * (j // 2) + 128]
            slab = jnp.where(low, slab, 0.0) if j % 2 == 0 else jnp.where(low, 0.0, slab)
            parts.append(slab.astype(BF))
    return jnp.concatenate(parts, axis=0)


def scores(i, q, qr, k, bias, ph):
    for b in range(2):
        qs = jnp.concatenate([queries(q, i, b), rotary(qr, i, b)], axis=1)
        s = dot(k[b], qs, NT) * SCALE + jnp.concatenate([bias[b]] * 4, axis=1)
        e = jnp.exp(s - jnp.max(s, axis=0, keepdims=True))
        ph[i, b] = (e * (1.0 / jnp.sum(e, axis=0, keepdims=True))).astype(BF)


def outputs(i, og, kt, ph, d):
    outs = [dot(kt[b], ph[i, b], NN).astype(BF) for b in range(2)]
    for pair in range(4):
        xh, part = pair // 2, pair % 2
        both = jnp.concatenate([out[:, 128 * pair : 128 * pair + 128] for out in outs], axis=1)
        dw = dot(both, grads_of_pair(og, i, xh, part), NN).astype(BF)
        for n, spot in enumerate(SPOTS):
            rows = dw[32 * n : 32 * n + 32]
            d[grad_at(part, xh, *spot, i)] = jnp.concatenate([rows[:, :HD], rows[:, HD:]], axis=0)


def backward(i, q, qr, og, k, w, ph, dk, dr):
    backs = []
    for pair in range(4):
        xh, part = pair // 2, pair % 2
        pieces = [w[weight_at(part, xh, *spot, i)] for spot in SPOTS]
        weight = jnp.concatenate(
            [jnp.concatenate([p[:32], p[32:]], axis=1) for p in pieces], axis=0
        )
        backs.append(dot(grads_of_pair(og, i, xh, part), weight, NT).astype(BF))
    for b in range(2):
        back = jnp.concatenate([back[128 * b : 128 * b + 128] for back in backs], axis=0)
        dp = dot(k[b, :, :LAT], back, NT)
        half = ph[i, b]
        prob = half.astype(F32)
        weighted = prob * dp
        delta = jnp.sum(weighted, axis=0, keepdims=True)
        ds = ((weighted - prob * delta) * SCALE).astype(BF)
        dk[b] += dot(
            jnp.concatenate([half, ds], axis=1), jnp.concatenate([back, queries(q, i, b)], axis=0), NN
        )
        dr[b] += dot(ds, rotary(qr, i, b), NN)


def core_kernel(
    ids, counts, cache, rope, w_in, q_hbm, qr_hbm, og_hbm, cg, rg, wg,
    kc, g, d, core_in, q, qr, og, rope_v, k, kt, bias, ph, dk, dr, drp, cin, p1, p2, q1, q2, zin,
    send, recv, lsem,
):
    x, y, z, core, xh = place()
    links = Links(send, recv)
    mine = (y, x)

    def own(n):
        return xh * 8 + (z + n + 8) % 8

    def oth(n):
        return (1 - xh) * 8 + (z + n + 8) % 8

    def upper(side):
        return pl.ds(HALF * side, HALF)

    first = [
        pltpu.make_async_copy(cache, kc.at[own(0), pl.ds(0, 12)], lsem.at[0]),
        pltpu.make_async_copy(rope, rope_v, lsem.at[1]),
        pltpu.make_async_copy(w_in, g.at[core, y, x, z], lsem.at[2]),
    ]
    loads = [
        pltpu.make_async_copy(qr_hbm, qr, lsem.at[4]),
        pltpu.make_async_copy(og_hbm, og, lsem.at[5]),
        pltpu.make_async_copy(q_hbm, q, lsem.at[6]),
    ]
    for copy in first:
        copy.start()
    links.barrier()
    for copy in first:
        copy.wait()
    flipped = jnp.concatenate([rope_v[...].astype(F32), jnp.zeros((ROPE, 64), F32)], axis=1)
    flipped = jnp.concatenate([flipped, jnp.zeros((128 - ROPE, 256), F32)], axis=0).T
    packed = [flipped[32 * i : 32 * i + 32, :ROPE].astype(BF) for i in range(6)]
    packed = jnp.concatenate(packed + [jnp.zeros((32, 128), BF)], axis=1)
    kc[own(0), 12] = packed[:16]
    kc[own(0), 13] = packed[16:]

    def ring_x(s):
        out = []
        for side, sign in ((0, 1), (1, -1)):
            if s == 1:
                ref = g.at[core, y, x]
            else:
                ref = g.at[core, y, (x - sign + 4) % 4, pl.ds(4 * side, 4)]
            out.append(links.push(ref, ref, "x", side))
        return out

    def ring_y1(n):
        ref = g.at[core, y, (x + n + 4) % 4]
        return [links.push(ref, ref, "y", side) for side in (0, 1)]

    def ring_y2(n, start=True):
        out = []
        for side, sign in ((0, 1), (1, -1)):
            ref = g.at[core, (y - sign + 4) % 4, (x + n + 4) % 4, pl.ds(4 * side, 4)]
            out.append(links.push(ref, ref, "y", side, start))
        return out

    shared = []

    def share(n, start=True):
        ref = g.at[core, (y + n) % 4]
        shared.append(links.push(ref, ref, "core", 0, start))
        return shared[-1]

    def share_far(n):
        ref = g.at[core, (y + 2) % 4, (x + n) % 4]
        shared.append(links.push(ref, ref, "core", 0, False))
        return shared[-1]

    def ring8(s):
        out = []
        for side, sign in ((0, 1), (1, -1)):
            ref = kc.at[own(-sign * (s - 1))]
            if s == 4:
                ref = ref.at[upper(side)]
            out.append(links.push(ref, ref, "z", side))
        return out

    def push_block(o, way, side=0, rows=None):
        ref = kc.at[o]
        if rows is not None:
            ref = ref.at[rows]
        return links.push(ref, ref, way, side)

    weights = g.at[core, y, x, z]
    c = ring8(1)
    cross0 = push_block(own(0), "far")
    wz = [links.push(weights, weights, ("z", n)) for n in (4, 3, 5, 2, 6, 1, 7)]
    arrive(c)
    c = ring8(2)
    for copy in loads:
        copy.start()
    arrive(wz)
    ya = ring_y1(0)
    wx = ring_x(1)
    arrive([cross0])
    near = [push_block(oth(0), "z", 0), push_block(oth(0), "z", 1)]
    arrive(c)
    c = ring8(3)
    cross2 = [push_block(own(2), "far"), push_block(own(-2), "far")]
    arrive(ya)
    ya2 = ring_y2(0)
    arrive(wx)
    wx = ring_x(2)
    yb = ring_y1(1) + ring_y1(-1)
    arrive(c)
    c = ring8(4)
    arrive(c)
    cross4 = push_block(own(4), "far")
    arrive(wx)
    yc = ring_y1(2)
    share(0)
    arrive(cross2)
    third = [push_block(oth(-2), "z", 0), push_block(oth(2), "z", 1)]
    arrive(yb)
    yb2 = ring_y2(1) + ring_y2(-1)
    row = lax.broadcasted_iota(jnp.int32, (256, 128), 0)
    col = lax.broadcasted_iota(jnp.int32, (256, 128), 1)
    for n in range(2):
        slot = row // 64
        causal = jnp.where(row % 64 <= col % 64, 0.0, -1e30).astype(F32)
        listed = jnp.where(slot < counts[n], 0.0, -1e30).astype(F32)
        bias[n] = jnp.where(slot == 0, causal, listed)
    dk[...] = jnp.zeros_like(dk)
    dr[...] = jnp.zeros_like(dr)
    for copy in loads:
        copy.wait()
    arrive(near)
    arrive([cross4])
    arrive(third)

    for n in range(2):
        for j in range(SEL):
            owner, part = lax.div(ids[n, j], 3), lax.rem(ids[n, j], 3)
            for r in range(4):
                k[n, 64 * j + 16 * r : 64 * j + 16 * r + 16, :LAT] = kc[owner, 4 * part + r]
            for r in range(2):
                packs = kc[owner, 12 + r].astype(F32)
                pack = packs[:, 256:384]
                pack = jnp.where(part == 0, packs[:, 0:128], pack)
                pack = jnp.where(part == 1, packs[:, 128:256], pack)
                low, high = pack[:, :64].astype(BF), pack[:, 64:].astype(BF)
                row = 64 * j + 16 * r
                k[n, row : row + 16, LAT:] = jnp.concatenate([low, low], axis=1)
                k[n, row + 32 : row + 48, LAT:] = jnp.concatenate([high, high], axis=1)
        kt[n] = k[n, :, :LAT].T

    first_swap = links.count
    links.count += 8

    def swap(i):
        return pltpu.make_async_remote_copy(
            src_ref=d.at[:, 1 - core, :, :, i],
            dst_ref=core_in.at[:, :, :, i],
            send_sem=send.at[first_swap + i],
            recv_sem=recv.at[first_swap + i],
            device_id=links.to["core"][0],
            device_id_type=MESH,
        )

    def add(dst, *srcs):
        total = dst[...].astype(F32)
        for src in srcs:
            total = total + src[...].astype(F32)
        dst[...] = total.astype(BF)

    def swap_add(i):
        swap(i).wait_recv()
        for part in (0, 1):
            for n in range(4):
                add(d.at[part, core, n, :, i], core_in.at[part, n, :, i])

    def p_send1(h, start=True):
        out = []
        for part, way in ((0, "y"), (1, "x")):
            for side in (0, 1):
                ref = d.at[part, core, (mine[part] + 2) % 4, pl.ds(2 * side, 2), pl.ds(4 * h, 4)]
                out.append(links.push(ref, p1.at[h, part, side], way, side, start))
        return out

    def p_add1(h):
        for part in (0, 1):
            for side, sign in ((0, 1), (1, -1)):
                o = (mine[part] + sign + 4) % 4
                for n in range(2):
                    add(d.at[part, core, o, 2 * side + n, pl.ds(4 * h, 4)], p1.at[h, part, side, n])

    def p_send2(h, start=True):
        out = []
        for part, way in ((0, "y"), (1, "x")):
            for side, sign in ((0, 1), (1, -1)):
                ref = d.at[part, core, (mine[part] + sign + 4) % 4, :, pl.ds(4 * h, 4)]
                out.append(links.push(ref, p2.at[h, part, side], way, side, start))
        return out

    def p_add2(h):
        for part in (0, 1):
            for n in range(4):
                ref = d.at[part, core, mine[part], n, pl.ds(4 * h, 4)]
                add(ref, p2.at[h, part, 0, n], p2.at[h, part, 1, n])

    def q_send1():
        out = []
        for part, way in ((0, "x"), (1, "y")):
            o = (mine[1 - part] + 2) % 4
            for side in (0, 1):
                rows = pl.ds(4 * side, 4)
                out.append(links.push(d.at[part, core, mine[part], o, rows], q1.at[part, side], way, side))
        return out

    def q_add1():
        for part in (0, 1):
            for side, sign in ((0, 1), (1, -1)):
                o = (mine[1 - part] + sign + 4) % 4
                add(d.at[part, core, mine[part], o, pl.ds(4 * side, 4)], q1.at[part, side])

    def q_send2():
        out = []
        for part, way in ((0, "x"), (1, "y")):
            for side, sign in ((0, 1), (1, -1)):
                o = (mine[1 - part] + sign + 4) % 4
                out.append(links.push(d.at[part, core, mine[part], o], q2.at[part, side], way, side))
        return out

    def q_add2():
        for part in (0, 1):
            add(d.at[part, core, mine[part], mine[1 - part]], q2.at[part, 0], q2.at[part, 1])

    def total_of(part):
        total = d[part, core, mine[part], mine[1 - part], z].astype(F32)
        for n in range(7):
            total = total + zin[part, n].astype(F32)
        return total

    yc2 = ring_y2(2, False)
    late = [share(1, False), share(3, False)] + [share_far(n) for n in (0, 1, 3, 2)]
    pa1 = p_send1(0, False)

    scores(0, q, qr, k, bias, ph)

    @pl.loop(1, 8)
    def _(i):
        scores(i, q, qr, k, bias, ph)
        outputs(i - 1, og, kt, ph, d)
        swap(i - 1).start()

        @pl.when(i > 1)
        def _():
            swap_add(i - 2)

        @pl.when(i == 1)
        def _():
            arrive(yc)
            for copy in yc2:
                copy.start()
            arrive(ya2)
            for copy in late[:3]:
                copy.start()

        @pl.when(i == 5)
        def _():
            for copy in pa1:
                copy.start()

        @pl.when(i == 4)
        def _():
            arrive(yb2)
            late[3].start()
            late[4].start()

    outputs(7, og, kt, ph, d)
    swap(7).start()
    swap_add(6)
    arrive(yc2)
    late[5].start()
    swap_add(7)
    pb1 = p_send1(1)
    arrive(shared)
    pa2, pb2 = p_send2(0, False), p_send2(1, False)

    @pl.loop(0, 8)
    def _(i):
        backward(i, q, qr, og, k, g, ph, dk, dr)

        @pl.when(i == 0)
        def _():
            arrive(pa1)
            p_add1(0)
            for copy in pa2:
                copy.start()

        @pl.when(i == 2)
        def _():
            arrive(pb1)
            p_add1(1)
            for copy in pb2:
                copy.start()

        @pl.when(i == 6)
        def _():
            arrive(pa2)
            p_add2(0)

    links.finish()
    links.started = []
    for n in range(2):
        for j in range(SEL):
            fold = dr[n, 64 * j : 64 * j + 64, :]
            fold = fold[:, :64] + fold[:, 64:]
            drp[SEL * n + j] = jnp.concatenate([fold[:32], fold[32:]], axis=1)

    def fill(o):
        hits = [
            [jnp.where(ids[n, j] == o * 3 + part, 1.0, 0.0).astype(F32) for n in range(2) for j in range(SEL)]
            for part in range(3)
        ]
        packs = []
        for part in range(3):
            pack = jnp.zeros((32, 128), F32)
            for n in range(2 * SEL):
                pack = pack + hits[part][n] * drp[n]
            packs.append(pack.astype(BF))
            for r in range(4):
                total = jnp.zeros((16, LAT), F32)
                for n in range(2 * SEL):
                    low = 64 * (n % SEL) + 16 * r
                    total = total + hits[part][n] * dk[n // SEL, low : low + 16, :]
                kc[o, 4 * part + r] = total.astype(BF)
        packs = jnp.concatenate(packs + [jnp.zeros((32, 128), BF)], axis=1)
        kc[o, 12] = packs[:16]
        kc[o, 13] = packs[16:]

    def away(o, slot, way, side=0, rows=None):
        src, dst = kc.at[o], cin.at[slot]
        if rows is not None:
            src, dst = src.at[rows], dst.at[rows]
        return links.push(src, dst, way, side)

    def take(o, slots, rows=slice(None)):
        total = kc[o, rows].astype(F32)
        for slot in slots:
            total = total + cin[slot, rows].astype(F32)
        kc[o, rows] = total.astype(BF)

    lower, higher = slice(0, HALF), slice(HALF, TILES)
    fill(oth(4))
    cross4 = away(oth(4), 0, "far")
    fill(oth(3))
    fill(oth(-3))
    third = [away(oth(3), 1, "z", 0), away(oth(-3), 2, "z", 1)]
    fill(oth(2))
    fill(oth(-2))
    fill(own(4))
    arrive(pb2)
    p_add2(1)
    w = q_send1()
    arrive(third)
    take(oth(2), [1])
    take(oth(-2), [2])
    cross2 = [away(oth(2), 3, "far"), away(oth(-2), 4, "far")]
    arrive([cross4])
    take(own(4), [0])
    c = [away(own(4), 5, "z", 0, upper(0)), away(own(4), 6, "z", 1, upper(1))]
    fill(own(3))
    fill(own(-3))
    arrive(c)
    take(own(3), [5], lower)
    take(own(-3), [6], higher)
    c = [away(own(3), 7, "z", 0), away(own(-3), 8, "z", 1)]
    arrive(w)
    q_add1()
    w = q_send2()
    fill(oth(1))
    fill(oth(-1))
    near = [away(oth(1), 9, "z", 0, upper(1)), away(oth(-1), 10, "z", 1, upper(0))]
    fill(own(2))
    fill(own(-2))
    fill(oth(0))
    cross1 = [away(oth(1), 11, "far", 0, upper(0)), away(oth(-1), 12, "far", 0, upper(1))]
    arrive(c)
    arrive(cross2)
    take(own(2), [7, 3])
    take(own(-2), [8, 4])
    c = [away(own(2), 13, "z", 0), away(own(-2), 14, "z", 1)]
    arrive(near)
    take(oth(0), [9], higher)
    take(oth(0), [10], lower)
    cross0 = away(oth(0), 15, "far")
    arrive(w)
    q_add2()
    w = [
        links.push(
            d.at[part, core, mine[part], mine[1 - part], (z + n) % 8], zin.at[part, n - 1], ("z", n)
        )
        for n in (4, 3, 5, 2, 6, 1, 7)
        for part in (0, 1)
    ]
    fill(own(1))
    fill(own(-1))
    fill(own(0))
    arrive(cross1)
    take(own(1), [11], lower)
    take(own(-1), [12], higher)
    arrive(c)
    take(own(1), [13])
    take(own(-1), [14])
    c = [away(own(1), 16, "z", 0), away(own(-1), 17, "z", 1)]
    arrive(w)
    wg[0:64, :] = total_of(0)
    wg[64:128, :] = total_of(1)
    arrive([cross0])
    arrive(c)
    total = kc[own(0)].astype(F32)
    for slot in (15, 16, 17):
        total = total + cin[slot].astype(F32)
    cg[...] = total[0:12].astype(BF)
    pack = total[12:14].reshape(32, LAT)
    rows = [pack[:, 64 * i : 64 * i + 64] for i in range(6)] + [jnp.zeros((64, ROPE), F32)]
    flipped = jnp.concatenate(rows, axis=0)
    flipped = jnp.concatenate([flipped, jnp.zeros((256, 128 - ROPE), F32)], axis=1).T
    rg[...] = flipped[:ROPE, :192].astype(BF)
    links.finish()

    @pl.loop(0, 8)
    def _(i):
        swap(i).wait_send()


def finish_kernel(cg, rg, wg, cg_out, rg_out, wg_out):
    cg_out[...] = cg[...]
    rg_out[...] = rg[...]
    wg_out[...] = wg[...]


def finish(*arrays):
    return pl.pallas_call(
        finish_kernel,
        out_shape=tuple(jax.ShapeDtypeStruct(a.shape, a.dtype) for a in arrays),
        in_specs=[pl.BlockSpec(memory_space=pltpu.VMEM)] * 3,
        out_specs=(pl.BlockSpec(memory_space=pltpu.VMEM),) * 3,
        name="finish",
    )(*arrays)


def run(ids, counts, cache, rope, weight, q, qr, og):
    return pl.pallas_call(
        core_kernel,
        out_shape=(
            jax.ShapeDtypeStruct((12, 16, LAT), BF),
            jax.ShapeDtypeStruct((ROPE, 192), BF),
            jax.ShapeDtypeStruct((128, HD), F32),
        ),
        in_specs=[pl.BlockSpec(memory_space=pltpu.SMEM)] * 2 + [pl.BlockSpec(memory_space=pl.ANY)] * 6,
        out_specs=(pl.BlockSpec(memory_space=pltpu.VMEM),) * 3,
        scratch_shapes=[
            pltpu.VMEM((16, TILES, 16, LAT), BF),
            pltpu.VMEM((2, 4, 4, 8, 128, HD), BF),
            pltpu.VMEM((2, 2, 4, 4, 8, 64, HD), BF),
            pltpu.VMEM((2, 4, 4, 8, 64, HD), BF),
            pltpu.VMEM((128, 64 * LAT), BF),
            pltpu.VMEM((128, 64 * ROPE), BF),
            pltpu.VMEM((128, 64 * HD), BF),
            pltpu.VMEM((ROPE, 192), BF),
            pltpu.VMEM((2, 256, LAT + 128), BF),
            pltpu.VMEM((2, LAT, 256), BF),
            pltpu.VMEM((2, 256, 128), F32),
            pltpu.VMEM((8, 2, 256, 512), BF),
            pltpu.VMEM((2, 256, LAT), F32),
            pltpu.VMEM((2, 256, 128), F32),
            pltpu.VMEM((2 * SEL, 32, 128), F32),
            pltpu.VMEM((18, TILES, 16, LAT), BF),
            pltpu.VMEM((2, 2, 2, 2, 4, 64, HD), BF),
            pltpu.VMEM((2, 2, 2, 4, 4, 64, HD), BF),
            pltpu.VMEM((2, 2, 4, 64, HD), BF),
            pltpu.VMEM((2, 2, 8, 64, HD), BF),
            pltpu.VMEM((2, 7, 64, HD), BF),
            pltpu.SemaphoreType.DMA((130,)),
            pltpu.SemaphoreType.DMA((130,)),
            pltpu.SemaphoreType.DMA((7,)),
        ],
        compiler_params=pltpu.CompilerParams(
            collective_id=0, has_side_effects=True, vmem_limit_bytes=63 * 2**20
        ),
        name="whole",
    )(ids, counts, cache, rope, weight, q, qr, og)


def shards(
    q_latent,
    q_rope,
    latent_cache,
    rope_keys,
    up_weight,
    out_grad,
    block_ids,
    block_counts,
    slab_offset,
):
    cg, rg, wg = finish(*run(
        block_ids[0],
        block_counts[0],
        latent_cache.reshape(12, 16, LAT),
        rope_keys[0].T,
        up_weight.reshape(128, HD),
        q_latent[0],
        q_rope[0],
        out_grad[0],
    ))
    return cg.reshape(1, 192, LAT), rg.T[None], wg.reshape(4, 32, HD)


def solution(mesh):
    placed = (
        P("dp", "ctx", None),
        P("dp", "ctx", None),
        P("dp", "ctx", None),
        P("dp", "ctx", None),
        P("ctx", "dp", None),
        P("dp", "ctx", None),
        P("dp", "ctx", None),
        P("dp", "ctx"),
        P("dp"),
    )
    return jax.shard_map(
        shards,
        mesh=mesh,
        in_specs=placed,
        out_specs=(P("dp", "ctx", None), P("dp", "ctx", None), P("ctx", "dp", None)),
        check_vma=False,
    )
```
